128 devices in a mesh: tp: 8 (over z, core), kv: 16 (over x, y).
Axes of the slice: x: 4, y: 4, z: 4, core: 2. Of those that a mesh axis runs over, the one named last changes fastest.
Arguments:
- tokens: bfloat16 [64, 8192], P(None, 'kv'), may hold values from -6 to 6
- gain: float32 [8192], P('kv'), may hold values from 0.1 to 1.9
- w_qkv: bfloat16 [8192, 8, 1280], P('kv', 'tp'), may hold values from -0.0625 to 0.0625
- w_out: bfloat16 [8, 1024, 8192], P('tp', None, 'kv'), may hold values from -0.0625 to 0.0625
- k_cache: bfloat16 [8, 160, 4096, 128], P('tp', 'kv')
- v_cache: bfloat16 [8, 160, 4096, 128], P('tp', 'kv'), may hold values from -12 to 12
- lengths: int32 [64], replicated, may hold values from 1 to 131072, as said below
- block_table: int32 [160, 2], P('kv'), may hold values from -1 to 63, as said below
Outputs:
- attn_proj: bfloat16 [64, 8192], P(None, 'kv')
The draws below stay inside these ranges and needn't reach their ends.
Inputs may be any that keep to these rules, and one draw needn't show every extreme that they name: `lengths`: every sequence has at least one cached token; exactly one sequence has 131072. `block_table`: entry [s, 0] is the sequence whose block sits in slot s and [s, 1] the block's place p in it (its tokens 4096 * p to 4096 * p + 4095); both are -1 for an empty slot. Each block that holds at least one cached token of a sequence sits in exactly one slot, and no other block is stored. On each index of kv the used slots come first; on some index all 10 slots are used.
All inputs are finite; a program needn't handle non-finite values.
Results may differ from the reference program's by a relative error of at most 0.0065.
The reference program's roundings to bfloat16 on the way count: a program that leaves them out, or rounds other values in their place, can miss the bound.
Values may be sent and summed in bfloat16 or wider, within the bound.
A program may use at most 128 MiB of HBM per device.

```python
import jax
import jax.numpy as jnp
from jax import lax

D = 8192
H = 64
KVH = 8
HD = 128
G = 8
BLK = 4096
MAXLEN = 131072
SLOTS = 10
ROWS = 64
SLOTS_ALL = 160


def block_layout(key):
    stored = MAXLEN // BLK
    spare_blocks = max(1, (SLOTS_ALL - stored) // max(ROWS - 1, 1))
    spare_blocks = min(spare_blocks, stored)
    long_row = jax.random.randint(jax.random.fold_in(key, 11), (), 0, ROWS)
    short_lengths = jax.random.randint(jax.random.fold_in(key, 12), (ROWS,), 1, spare_blocks * BLK + 1)
    row_numbers = jnp.arange(ROWS, dtype=jnp.int32)
    lengths = jnp.where(row_numbers == long_row, MAXLEN, short_lengths).astype(jnp.int32)
    block_counts = (lengths + BLK - 1) // BLK
    row_order = jax.random.permutation(jax.random.fold_in(key, 13), ROWS).astype(jnp.int32)
    holder_order = jax.random.permutation(jax.random.fold_in(key, 14), SLOTS_ALL // SLOTS).astype(jnp.int32)
    row_grid = jnp.broadcast_to(row_order[:, None], (ROWS, stored))
    place_grid = jnp.broadcast_to(jnp.arange(stored, dtype=jnp.int32)[None, :], (ROWS, stored))
    used_flags = (place_grid < block_counts[row_grid]).reshape(-1).astype(jnp.int32)
    ranking = jnp.cumsum(used_flags) - 1
    ranking = jnp.maximum(ranking, 0)
    targets = holder_order[ranking // SLOTS] * SLOTS + ranking % SLOTS
    targets = jnp.where(used_flags > 0, targets, SLOTS_ALL).astype(jnp.int32)
    entries = jnp.stack([row_grid.reshape(-1), place_grid.reshape(-1)], axis=1).astype(jnp.int32)
    table_values = jnp.full((SLOTS_ALL, 2), -1, jnp.int32).at[targets].set(entries, mode='drop')
    return (lengths, table_values)


def draw_lengths(key, part):
    return block_layout(key)[0]


def draw_block_table(key, part):
    return block_layout(key)[1]


def draw_k_cache(key, part):
    key = jax.random.fold_in(key, 5)
    array_shape = (KVH, SLOTS_ALL, BLK, HD)
    values_base = jax.random.normal(jax.random.fold_in(key, 1), array_shape, jnp.float32)
    values_base = jnp.clip(values_base, -5.0, 5.0)
    return values_base.astype(jnp.bfloat16)


def block_levels(stream_key, extent, shards, low, largest):
    loudness, own = 1.0, jax.random.fold_in(stream_key, 6)
    for dim, blocks in shards:
        steps = jnp.exp(jax.random.uniform(jax.random.fold_in(own, dim), (blocks,), jnp.float32, low / len(shards), largest / len(shards)))
        loudness = loudness * jnp.repeat(steps, extent[dim] // blocks).reshape([-1 if axis == dim else 1 for axis in range(len(extent))])
    return loudness


def scatter_about(key, shape, spread, bound, split=(), kind=jnp.bfloat16):
    drawn = spread * jax.random.normal(key, shape, jnp.float32)
    if split:
        drawn = drawn * block_levels(key, shape, split, -0.22, 0.18)
    return jnp.clip(drawn, -bound, bound).astype(kind)


def setup_inputs(seed: int = 0) -> dict:
    splits = jax.random.split(jax.random.key(seed), 9)
    tokens = scatter_about(splits[0], (ROWS, D), 1.0, 6.0, ((1, 16),))
    gain = jnp.clip(1.0 + 0.18 * jax.random.normal(splits[1], (D,), jnp.float32), 0.1, 1.9)
    w_qkv = scatter_about(splits[2], (D, KVH, (G + 2) * HD), D ** -0.5, 0.0625, ((0, 16), (1, 8)))
    w_out = scatter_about(splits[3], (KVH, G * HD, D), (H * HD) ** -0.5, 0.0625, ((0, 8), (2, 16)))
    k_cache = draw_k_cache(jax.random.fold_in(splits[8], 71), 0)
    v_cache = scatter_about(splits[5], (KVH, SLOTS_ALL, BLK, HD), 2.0, 12.0, ((0, 8), (1, 16)))
    lengths = draw_lengths(jax.random.fold_in(splits[8], 71), 0)
    block_table = draw_block_table(jax.random.fold_in(splits[8], 71), 0)
    return dict(tokens=tokens, gain=gain, w_qkv=w_qkv, w_out=w_out, k_cache=k_cache, v_cache=v_cache, lengths=lengths, block_table=block_table)


epsilon = 1e-05
floor_score = -1e+30

def reference(tokens, gain, w_qkv, w_out, k_cache, v_cache, lengths, block_table):
    wide_tokens = tokens.astype(jnp.float32)
    mean_square = lax.optimization_barrier(jnp.mean(wide_tokens * wide_tokens, axis=1, keepdims=True))
    normed = (wide_tokens * lax.rsqrt(mean_square + epsilon) * gain[None, :]).astype(jnp.bfloat16)
    projected = jnp.dot(normed, w_qkv.reshape(D, KVH * (G + 2) * HD), preferred_element_type=jnp.float32).astype(jnp.bfloat16)
    projected = lax.optimization_barrier(projected).reshape(ROWS, KVH, G + 2, HD)
    queries = projected[:, :, :G].astype(jnp.float32)
    new_keys = projected[:, :, G].astype(jnp.float32)
    new_values = projected[:, :, G + 1].astype(jnp.float32)
    score_scale = HD ** (-0.5)
    offsets = jnp.arange(BLK, dtype=jnp.int32)

    def slot_terms(slot_index):
        owner_row = jnp.maximum(block_table[slot_index, 0], 0)
        start_token = block_table[slot_index, 1] * BLK
        query_rows = lax.dynamic_index_in_dim(queries, owner_row, 0, keepdims=False)
        key_block = lax.dynamic_index_in_dim(k_cache, slot_index, 1, keepdims=False).astype(jnp.float32)
        value_block = lax.dynamic_index_in_dim(v_cache, slot_index, 1, keepdims=False).astype(jnp.float32)
        scores = jnp.einsum('hgd,hjd->hgj', query_rows, key_block, precision=lax.Precision.HIGHEST) * score_scale
        visible = start_token + offsets < lengths[owner_row]
        scores = jnp.where(visible[None, None, :], scores, floor_score)
        block_top = lax.optimization_barrier(jnp.max(scores, axis=-1))
        weights = jnp.exp(scores - block_top[..., None])
        block_total = lax.optimization_barrier(jnp.sum(weights, axis=-1))
        rounded = lax.optimization_barrier(weights.astype(jnp.bfloat16)).astype(jnp.float32)
        block_out = jnp.einsum('hgj,hjd->hgd', rounded, value_block, precision=lax.Precision.HIGHEST)
        return (block_top, block_total, block_out)
    slot_ids = jnp.arange(SLOTS_ALL, dtype=jnp.int32)
    block_tops, block_totals, block_outs = lax.map(slot_terms, slot_ids)
    segment_ids = jnp.where(block_table[:, 0] >= 0, block_table[:, 0], ROWS).astype(jnp.int32)
    highest_all = jax.ops.segment_max(block_tops, segment_ids, num_segments=ROWS + 1)
    factors = jnp.exp(block_tops - highest_all[segment_ids])
    weight_sums = jax.ops.segment_sum(block_totals * factors, segment_ids, num_segments=ROWS + 1)[:ROWS]
    weighted = jax.ops.segment_sum(block_outs * factors[..., None], segment_ids, num_segments=ROWS + 1)[:ROWS]
    cache_top = highest_all[:ROWS]
    own_scores = lax.optimization_barrier(jnp.sum(queries * new_keys[:, :, None, :], axis=-1)) * score_scale
    highest = jnp.maximum(cache_top, own_scores)
    cache_factor = jnp.exp(cache_top - highest)
    own_weight = jnp.exp(own_scores - highest)
    denominator = weight_sums * cache_factor + own_weight
    numerator = weighted * cache_factor[..., None] + own_weight[..., None] * new_values[:, :, None, :]
    attended = (numerator / denominator[..., None]).astype(jnp.bfloat16)
    flattened = attended.reshape(ROWS, H * HD)
    result = jnp.dot(flattened, w_out.reshape(H * HD, D), preferred_element_type=jnp.float32)
    return result.astype(jnp.bfloat16)
```

```python
import functools

import jax
import jax.numpy as jnp
from jax import lax
from jax.experimental import pallas as pl
from jax.experimental.pallas import tpu as pltpu
from jax.sharding import PartitionSpec as P

D = 8192
HD = 128
G = 8
ROWS = 64
SLOTS = 10
ENTRIES = G + 2
BLK = 4096
SIDE = 4
KV = SIDE * SIDE
PEERS = KV - 1
HALF = 256

EPSILON = 1e-05
FLOOR = -1e30
SCALE = HD ** (-0.5)

MESH = pl.DeviceIdType.MESH
F32 = jnp.float32
BF16 = jnp.bfloat16
NT = (((1,), (1,)), ((), ()))

CHUNKS = ((0, 4, 40), (4, 4, 40), (8, 2, 24))


def ring_distance(step):
    return min(step, SIDE - step)


OFFSETS = sorted(
    [(a, b) for a in range(SIDE) for b in range(SIDE) if (a, b) != (0, 0)],
    key=lambda m: -(ring_distance(m[0]) + ring_distance(m[1])),
)


def wait_bytes(ref, sem):
    pltpu.make_async_copy(ref, ref, sem).wait()


def kernel(
    tokens_hbm,
    gain_hbm,
    w_qkv_hbm,
    w_out_hbm,
    k_hbm,
    v_hbm,
    lengths,
    table,
    out_ref,
    tokens_v,
    gain_v,
    w_qkv,
    w_out,
    k_v,
    v_v,
    first_all,
    send0,
    send1,
    send2,
    recv0,
    recv1,
    recv2,
    query_rows,
    outs_all,
    stats_all,
    outs_wide,
    half_send,
    half_recv,
    z_all,
    done_send,
    done_recv,
    load_sem,
    kv_sem,
    send_sem,
    recv_sem,
):
    me = lax.axis_index("kv")
    my_x, my_y = me // SIDE, me % SIDE
    tp = lax.axis_index("tp")
    my_z, core = tp // 2, tp % 2

    def ahead(offset):
        return {"kv": ((my_x + offset[0]) % SIDE) * SIDE + (my_y + offset[1]) % SIDE}

    def behind(offset):
        return ahead(((SIDE - offset[0]) % SIDE, (SIDE - offset[1]) % SIDE))

    sibling = {"tp": my_z * 2 + (1 - core)}
    z_peers = [{"tp": ((my_z + step) % SIDE) * 2 + core} for step in (2, 1, 3)]

    barrier = pltpu.get_barrier_semaphore()
    for offset in OFFSETS:
        pl.semaphore_signal(barrier, inc=1, device_id=ahead(offset), device_id_type=MESH)
    for peer in z_peers + [sibling]:
        pl.semaphore_signal(barrier, inc=1, device_id=peer, device_id_type=MESH)

    loads = [
        pltpu.make_async_copy(tokens_hbm, tokens_v, load_sem.at[0]),
        pltpu.make_async_copy(gain_hbm, gain_v, load_sem.at[1]),
        pltpu.make_async_copy(w_qkv_hbm, w_qkv, load_sem.at[2]),
        pltpu.make_async_copy(w_out_hbm, w_out, load_sem.at[3]),
    ]
    k_loads, v_loads = [], []
    for pair in range(SLOTS // 2):
        part = pl.ds(2 * pair, 2)
        k_loads.append(pltpu.make_async_copy(k_hbm.at[part], k_v.at[part], kv_sem.at[0, pair]))
        v_loads.append(pltpu.make_async_copy(v_hbm.at[part], v_v.at[part], kv_sem.at[1, pair]))
    for load in loads[:3]:
        load.start()
    for pair in range(SLOTS // 2):
        k_loads[pair].start()
        v_loads[pair].start()
    loads[3].start()

    sub = lax.broadcasted_iota(jnp.int32, (8, HD), 0)
    lane = lax.broadcasted_iota(jnp.int32, (8, HD), 1)

    loads[0].wait()
    tokens = tokens_v[...].astype(F32)
    squares = jnp.sum(tokens * tokens, axis=1, keepdims=True)
    tile = jnp.zeros((8, HD), F32)
    for k in range(ROWS // 8):
        tile = jnp.where(lane == k, squares[8 * k : 8 * k + 8], tile)
    first_all[PEERS, 0:8, :] = tile
    for c, (start, count, _) in enumerate(CHUNKS):
        owners = jnp.full((8, HD), -1, jnp.int32)
        for s in range(count):
            owners = jnp.where(sub % count == s, table[0, start + s], owners)
        first_all[PEERS, 8 + 8 * c : 16 + 8 * c, :] = owners.astype(F32)
    owners = jnp.full((8, HD), -1, jnp.int32)
    for s in range(SLOTS):
        owners = jnp.where(lane == s, table[0, s], owners)
    first_all[PEERS, 32:40, :] = owners.astype(F32)

    pl.semaphore_wait(barrier, PEERS + 4)

    def send(phase, src, dst, peer):
        pltpu.make_async_remote_copy(
            src_ref=src,
            dst_ref=dst,
            send_sem=send_sem.at[phase],
            recv_sem=recv_sem.at[phase],
            device_id=peer,
            device_id_type=MESH,
        ).start()

    others = pl.ds(0, PEERS)

    for j, offset in enumerate(OFFSETS):
        send(0, first_all.at[PEERS], first_all.at[j], ahead(offset))
    loads[1].wait()
    loads[2].wait()
    wait_bytes(first_all.at[others], recv_sem.at[0])

    squares = first_all[0, 0:8, :]
    for j in range(1, KV):
        squares = squares + first_all[j, 0:8, :]
    inverse = lax.rsqrt(squares / D + EPSILON)
    gains = gain_v[...]
    normed = jnp.concatenate(
        [tokens[8 * k : 8 * k + 8] * inverse[:, k : k + 1] * gains for k in range(ROWS // 8)], axis=0
    ).astype(BF16)
    partial = jnp.dot(normed, w_qkv[...], preferred_element_type=F32)
    high = partial.astype(BF16)
    rest = partial - high.astype(F32)
    middle = rest.astype(BF16)
    low = (rest - middle.astype(F32)).astype(BF16)
    stacked = jnp.concatenate([high, middle, low, jnp.zeros_like(low)], axis=0)

    row_of_lane = lax.broadcasted_iota(jnp.int32, (KV * 8, HD), 1)
    row_number = (row_of_lane % ROWS).astype(F32)
    sub3 = lax.broadcasted_iota(jnp.int32, (KV, 8, HD), 1)
    sends = (send0, send1, send2)
    recvs = (recv0, recv1, recv2)
    for c, (start, count, rows) in enumerate(CHUNKS):
        owners = first_all[:, 8 + 8 * c : 16 + 8 * c, :].reshape(KV * 8, HD)
        hit = jnp.where(owners == row_number, 1.0, 0.0)
        pick = jnp.concatenate([hit, jnp.where(row_of_lane < ROWS, hit, 0.0)], axis=1).astype(BF16)
        packed = jnp.dot(pick, stacked, preferred_element_type=F32).reshape(KV, 8, ENTRIES * HD)
        per_tile = 8 // count
        for k in range(rows // 8):
            tile = packed[:, :, per_tile * k * HD : (per_tile * k + 1) * HD]
            for e in range(1, per_tile):
                entry = per_tile * k + e
                if entry < ENTRIES:
                    tile = jnp.where(
                        sub3 >= e * count, packed[:, :, entry * HD : (entry + 1) * HD], tile
                    )
            sends[c][:, 8 * k : 8 * k + 8, :] = tile
        for j, offset in enumerate(OFFSETS):
            send(1 + c, sends[c].at[j], recvs[c].at[j], behind(offset))

    sub16 = lax.broadcasted_iota(jnp.int32, (16, HD), 0)
    column = lax.broadcasted_iota(jnp.int32, (16, 1), 0)
    position = lax.broadcasted_iota(jnp.int32, (16, BLK), 1)
    stats = jnp.zeros((8, HD), F32)

    for c, (start, count, rows) in enumerate(CHUNKS):
        wait_bytes(recvs[c].at[others], recv_sem.at[1 + c])
        total = sends[c][PEERS]
        for j in range(PEERS):
            total = total + recvs[c][j]
        total = total.astype(BF16).astype(F32)
        per_tile = 8 // count
        for entry in range(ENTRIES):
            row = entry * count
            query_rows[pl.ds(16 * start + entry, count, stride=16), :] = total[row : row + count]

        for pair in range(start // 2, (start + count) // 2):
            a, b = 2 * pair, 2 * pair + 1
            k_loads[pair].wait()
            v_loads[pair].wait()
            queries = jnp.concatenate(
                [query_rows[16 * a : 16 * a + 8, :], query_rows[16 * b : 16 * b + 8, :]], axis=0
            )
            new_keys = jnp.where(
                sub16 < 8, query_rows[16 * a + 8 : 16 * a + 9, :], query_rows[16 * b + 8 : 16 * b + 9, :]
            )
            new_values = jnp.where(
                sub16 < 8, query_rows[16 * a + 9 : 16 * a + 10, :], query_rows[16 * b + 9 : 16 * b + 10, :]
            )
            left = jnp.concatenate(
                [jnp.where(sub16 < 8, queries, 0.0), jnp.where(sub16 < 8, 0.0, queries)], axis=1
            ).astype(BF16)
            keys = jnp.concatenate([k_v[a], k_v[b]], axis=1)
            scores = lax.dot_general(left, keys, NT, preferred_element_type=F32) * SCALE
            limit_a = lengths[jnp.maximum(table[0, a], 0)] - BLK * table[1, a]
            limit_b = lengths[jnp.maximum(table[0, b], 0)] - BLK * table[1, b]
            limit = jnp.where(column < 8, limit_a, limit_b)
            scores = jnp.where(position < limit, scores, FLOOR)
            top = jnp.max(scores, axis=1, keepdims=True)
            weights = jnp.exp(scores - top)
            block_total = jnp.sum(weights, axis=1, keepdims=True)
            values = jnp.concatenate([v_v[a], v_v[b]], axis=1)
            both = jnp.dot(weights.astype(BF16), values, preferred_element_type=F32)
            block_out = jnp.where(sub16 < 8, both[:, :HD], both[:, HD:])

            is_first = jnp.where(column < 8, table[1, a], table[1, b]) == 0
            own = jnp.sum(queries * new_keys, axis=1, keepdims=True) * SCALE
            own = jnp.where(is_first, own, FLOOR)
            highest = jnp.maximum(top, own)
            factor = jnp.exp(top - highest)
            own_weight = jnp.where(is_first, jnp.exp(own - highest), 0.0)
            slot_total = block_total * factor + own_weight
            slot_out = (block_out * factor + own_weight * new_values) / slot_total
            outs_all[PEERS, 16 * pair : 16 * pair + 16, :] = slot_out.astype(BF16)
            for s, part in ((a, slice(0, 8)), (b, slice(8, 16))):
                stats = jnp.where(lane == s, highest[part], stats)
                stats = jnp.where(lane == 16 + s, slot_total[part], stats)
        part = pl.ds(8 * start, 8 * count)
        for j, offset in enumerate(OFFSETS):
            send(4 + c, outs_all.at[PEERS, part], outs_all.at[j, part], ahead(offset))
    stats_all[PEERS] = stats
    for j, offset in enumerate(OFFSETS):
        send(7, stats_all.at[PEERS], stats_all.at[j], ahead(offset))

    def side_by_side(tiles, shift):
        near = jnp.full((8, HD), -1.0, F32)
        far = jnp.full((8, HD), -1.0, F32)
        for j in range(KV):
            at = SLOTS * j
            moved = pltpu.roll(tiles(j), (at - shift) % HD, 1)
            if at < HD:
                near = jnp.where((lane >= at) & (lane < at + SLOTS), moved, near)
            if at + SLOTS > HD:
                far = jnp.where((lane >= at - HD) & (lane < at + SLOTS - HD), moved, far)
        return jnp.concatenate([near, far], axis=1)

    owners = side_by_side(lambda j: first_all[j, 32:40, :], 0)
    belongs = lax.broadcasted_iota(jnp.int32, (ROWS, 2 * HD), 0).astype(F32) == owners[0:1]

    wait_bytes(stats_all.at[others], recv_sem.at[7])
    tops = side_by_side(lambda j: stats_all[j], 0)
    totals = side_by_side(lambda j: stats_all[j], 16)
    shares = []
    for g in range(G):
        masked = jnp.where(belongs, tops[g : g + 1], -3e38)
        highest = jnp.max(masked, axis=1, keepdims=True)
        share = jnp.where(belongs, jnp.exp(masked - highest) * totals[g : g + 1], 0.0)
        share = share / jnp.sum(share, axis=1, keepdims=True)
        upper = share.astype(BF16)
        lower = (share - upper.astype(F32)).astype(BF16)
        shares.append(jnp.concatenate([upper, lower], axis=0))

    for c, (start, count, rows) in enumerate(CHUNKS):
        wait_bytes(outs_all.at[others, pl.ds(8 * start, 8 * count)], recv_sem.at[4 + c])
    outs_wide[...] = outs_all[...].astype(F32).reshape(KV * SLOTS * G, HD)
    attended = []
    for g in range(G):
        slots = outs_wide[pl.ds(g, KV * SLOTS, stride=G), :].astype(BF16)
        slots = jnp.concatenate([slots, jnp.zeros((2 * HD - KV * SLOTS, HD), BF16)], axis=0)
        both = jnp.dot(shares[g], slots, preferred_element_type=F32)
        attended.append((both[:ROWS] + both[ROWS:]).astype(BF16))
    attended = jnp.concatenate(attended, axis=1)

    loads[3].wait()
    mine = pl.ds(pl.multiple_of(core * HALF, HALF), HALF)
    theirs = pl.ds(pl.multiple_of((1 - core) * HALF, HALF), HALF)
    half_send[...] = jnp.dot(attended, w_out[:, theirs], preferred_element_type=F32)
    send(8, half_send, half_recv, sibling)
    own_half = jnp.dot(attended, w_out[:, mine], preferred_element_type=F32)
    wait_bytes(half_recv, recv_sem.at[8])
    z_all[my_z] = own_half + half_recv[...]
    for peer in z_peers:
        send(9, z_all.at[my_z], z_all.at[my_z], peer)
    wait_bytes(z_all.at[pl.ds(0, SIDE - 1)], recv_sem.at[9])
    done = (((z_all[0] + z_all[1]) + z_all[2]) + z_all[3]).astype(BF16)
    done_send[...] = done
    send(10, done_send, done_recv, sibling)
    out_ref[:, mine] = done
    wait_bytes(done_recv, recv_sem.at[10])
    out_ref[:, theirs] = done_recv[...]

    wait_bytes(first_all.at[others], send_sem.at[0])
    for c, (start, count, rows) in enumerate(CHUNKS):
        wait_bytes(sends[c].at[others], send_sem.at[1 + c])
        wait_bytes(outs_all.at[others, pl.ds(8 * start, 8 * count)], send_sem.at[4 + c])
    wait_bytes(stats_all.at[others], send_sem.at[7])
    wait_bytes(half_send, send_sem.at[8])
    wait_bytes(z_all.at[pl.ds(0, SIDE - 1)], send_sem.at[9])
    wait_bytes(done_send, send_sem.at[10])


def per_device(tokens, gain, w_qkv, w_out, k_cache, v_cache, lengths, block_table):
    features = tokens.shape[1]
    anywhere = pl.BlockSpec(memory_space=pl.ANY)
    scalars = pl.BlockSpec(memory_space=pltpu.SMEM)
    return pl.pallas_call(
        kernel,
        out_shape=jax.ShapeDtypeStruct((ROWS, features), BF16),
        in_specs=[anywhere] * 6 + [scalars] * 2,
        out_specs=pl.BlockSpec(memory_space=pltpu.VMEM),
        scratch_shapes=[
            pltpu.VMEM((ROWS, features), BF16),
            pltpu.VMEM((1, features), F32),
            pltpu.VMEM((features, ENTRIES * HD), BF16),
            pltpu.VMEM((G * HD, features), BF16),
            pltpu.VMEM((SLOTS, BLK, HD), BF16),
            pltpu.VMEM((SLOTS, BLK, HD), BF16),
            pltpu.VMEM((KV, 40, HD), F32),
        ]
        + [pltpu.VMEM((KV, rows, HD), F32) for _, _, rows in CHUNKS]
        + [pltpu.VMEM((PEERS, rows, HD), F32) for _, _, rows in CHUNKS]
        + [
            pltpu.VMEM((SLOTS * 16, HD), F32),
            pltpu.VMEM((KV, SLOTS * G, HD), BF16),
            pltpu.VMEM((KV, 8, HD), F32),
            pltpu.VMEM((KV * SLOTS * G, HD), F32),
            pltpu.VMEM((ROWS, HALF), F32),
            pltpu.VMEM((ROWS, HALF), F32),
            pltpu.VMEM((SIDE, ROWS, HALF), F32),
            pltpu.VMEM((ROWS, HALF), BF16),
            pltpu.VMEM((ROWS, HALF), BF16),
            pltpu.SemaphoreType.DMA((4,)),
            pltpu.SemaphoreType.DMA((2, SLOTS // 2)),
            pltpu.SemaphoreType.DMA((11,)),
            pltpu.SemaphoreType.DMA((11,)),
        ],
        compiler_params=pltpu.CompilerParams(
            collective_id=0, has_side_effects=True, vmem_limit_bytes=56 << 20
        ),
    )(
        tokens,
        gain.reshape(1, features),
        w_qkv.reshape(features, ENTRIES * HD),
        w_out.reshape(G * HD, features),
        k_cache.reshape(SLOTS, BLK, HD),
        v_cache.reshape(SLOTS, BLK, HD),
        lengths,
        block_table.T,
    )


def solution(mesh):
    placed = (
        P(None, "kv"),
        P("kv"),
        P("kv", "tp", None),
        P("tp", None, "kv"),
        P("tp", "kv", None, None),
        P("tp", "kv", None, None),
        P(),
        P("kv", None),
    )
    return jax.shard_map(
        per_device, mesh=mesh, in_specs=placed, out_specs=P(None, "kv"), check_vma=False
    )
```

```python
import functools

import jax
import jax.numpy as jnp
from jax import lax
from jax.experimental import pallas as pl
from jax.experimental.pallas import tpu as pltpu
from jax.sharding import PartitionSpec as P

D = 8192
HD = 128
G = 8
ROWS = 64
SLOTS = 10
ENTRIES = G + 2
BLK = 4096
SIDE = 4
KV = SIDE * SIDE
PEERS = KV - 1
HALF = 256

EPSILON = 1e-05
FLOOR = -1e30
SCALE = HD ** (-0.5)

MESH = pl.DeviceIdType.MESH
F32 = jnp.float32
BF16 = jnp.bfloat16
NT = (((1,), (1,)), ((), ()))

SQUARE_LANE = 8
OWNER_LANE = 16

EARLY_PAIRS = 3
CHUNKS = ((0, 4, 40), (4, 4, 40), (8, 2, 24))


def ring_distance(step):
    return min(step, SIDE - step)


OFFSETS = sorted(
    [(a, b) for a in range(SIDE) for b in range(SIDE) if (a, b) != (0, 0)],
    key=lambda m: -(ring_distance(m[0]) + ring_distance(m[1])),
)


def wait_bytes(ref, sem):
    pltpu.make_async_copy(ref, ref, sem).wait()


def kernel(
    tokens_hbm,
    gain_hbm,
    w_qkv_hbm,
    w_out_hbm,
    k_hbm,
    v_hbm,
    lengths_hbm,
    table_hbm,
    out_ref,
    tokens_v,
    gain_v,
    w_qkv,
    w_out,
    k_v,
    v_v,
    first_all,
    send0,
    send1,
    send2,
    recv0,
    recv1,
    recv2,
    query_rows,
    outs_all,
    stats_all,
    outs_wide,
    half_send,
    half_recv,
    z_all,
    done_send,
    done_recv,
    lengths,
    table,
    load_sem,
    kv_sem,
    send_sem,
    recv_sem,
):
    me = lax.axis_index("kv")
    my_x, my_y = me // SIDE, me % SIDE
    tp = lax.axis_index("tp")
    my_z, core = tp // 2, tp % 2

    def ahead(offset):
        return {"kv": ((my_x + offset[0]) % SIDE) * SIDE + (my_y + offset[1]) % SIDE}

    def behind(offset):
        return ahead(((SIDE - offset[0]) % SIDE, (SIDE - offset[1]) % SIDE))

    sibling = {"tp": my_z * 2 + (1 - core)}
    z_peers = [{"tp": ((my_z + step) % SIDE) * 2 + core} for step in (2, 1, 3)]

    barrier = pltpu.get_barrier_semaphore()
    for offset in OFFSETS:
        pl.semaphore_signal(barrier, inc=1, device_id=ahead(offset), device_id_type=MESH)
    for peer in z_peers + [sibling]:
        pl.semaphore_signal(barrier, inc=1, device_id=peer, device_id_type=MESH)

    loads = [
        pltpu.make_async_copy(tokens_hbm, tokens_v, load_sem.at[0]),
        pltpu.make_async_copy(gain_hbm, gain_v, load_sem.at[1]),
        pltpu.make_async_copy(w_qkv_hbm, w_qkv, load_sem.at[2]),
        pltpu.make_async_copy(w_out_hbm, w_out, load_sem.at[3]),
        pltpu.make_async_copy(table_hbm, table, load_sem.at[4]),
        pltpu.make_async_copy(lengths_hbm, lengths, load_sem.at[5]),
    ]
    k_loads, v_loads = [], []
    for pair in range(SLOTS // 2):
        part = pl.ds(2 * pair, 2)
        k_loads.append(pltpu.make_async_copy(k_hbm.at[part], k_v.at[part], kv_sem.at[0, pair]))
        v_loads.append(pltpu.make_async_copy(v_hbm.at[part], v_v.at[part], kv_sem.at[1, pair]))
    for load in loads[:3] + loads[4:]:
        load.start()
    for pair in range(EARLY_PAIRS):
        k_loads[pair].start()
        v_loads[pair].start()

    sub = lax.broadcasted_iota(jnp.int32, (8, HD), 0)
    lane = lax.broadcasted_iota(jnp.int32, (8, HD), 1)

    loads[0].wait()
    tokens = tokens_v[...].astype(F32)
    squares = jnp.sum(tokens * tokens, axis=1, keepdims=True)
    loads[4].wait()
    loads[5].wait()
    owners = jnp.full((8, HD), -1, jnp.int32)
    for slot in range(SLOTS):
        owners = jnp.where(lane == OWNER_LANE + slot, table[0, slot], owners)
    for c, (start, count, _) in enumerate(CHUNKS):
        for s in range(count):
            owners = jnp.where((lane == c) & (sub % count == s), table[0, start + s], owners)
    tile = owners.astype(F32)
    for k in range(ROWS // 8):
        tile = jnp.where(lane == SQUARE_LANE + k, squares[8 * k : 8 * k + 8], tile)
    first_all[PEERS] = tile

    pl.semaphore_wait(barrier, PEERS + 4)

    def send(phase, src, dst, peer):
        pltpu.make_async_remote_copy(
            src_ref=src,
            dst_ref=dst,
            send_sem=send_sem.at[phase],
            recv_sem=recv_sem.at[phase],
            device_id=peer,
            device_id_type=MESH,
        ).start()

    others = pl.ds(0, PEERS)

    for j, offset in enumerate(OFFSETS):
        send(0, first_all.at[PEERS], first_all.at[j], ahead(offset))
    loads[1].wait()
    loads[2].wait()
    wait_bytes(first_all.at[others], recv_sem.at[0])

    for pair in range(EARLY_PAIRS, SLOTS // 2):
        k_loads[pair].start()
        v_loads[pair].start()
    loads[3].start()
    squares = first_all[0]
    for j in range(1, KV):
        squares = squares + first_all[j]
    inverse = lax.rsqrt(squares / D + EPSILON)
    gains = gain_v[...]
    normed = jnp.concatenate(
        [tokens[8 * k : 8 * k + 8] * inverse[:, SQUARE_LANE + k : SQUARE_LANE + k + 1] * gains for k in range(ROWS // 8)], axis=0
    ).astype(BF16)
    partial = jnp.dot(normed, w_qkv[...], preferred_element_type=F32)
    high = partial.astype(BF16)
    rest = partial - high.astype(F32)
    middle = rest.astype(BF16)
    low = (rest - middle.astype(F32)).astype(BF16)
    stacked = jnp.concatenate([high, middle, low, jnp.zeros_like(low)], axis=0)

    row_of_lane = lax.broadcasted_iota(jnp.int32, (KV * 8, HD), 1)
    row_number = (row_of_lane % ROWS).astype(F32)
    everyone = first_all[...].reshape(KV * 8, HD)
    sub3 = lax.broadcasted_iota(jnp.int32, (KV, 8, HD), 1)
    sends = (send0, send1, send2)
    recvs = (recv0, recv1, recv2)
    for c, (start, count, rows) in enumerate(CHUNKS):
        hit = jnp.where(everyone[:, c : c + 1] == row_number, 1.0, 0.0)
        pick = jnp.concatenate([hit, jnp.where(row_of_lane < ROWS, hit, 0.0)], axis=1).astype(BF16)
        packed = jnp.dot(pick, stacked, preferred_element_type=F32).reshape(KV, 8, ENTRIES * HD)
        per_tile = 8 // count
        for k in range(rows // 8):
            tile = packed[:, :, per_tile * k * HD : (per_tile * k + 1) * HD]
            for e in range(1, per_tile):
                entry = per_tile * k + e
                if entry < ENTRIES:
                    tile = jnp.where(
                        sub3 >= e * count, packed[:, :, entry * HD : (entry + 1) * HD], tile
                    )
            sends[c][:, 8 * k : 8 * k + 8, :] = tile
        for j, offset in enumerate(OFFSETS):
            send(1 + c, sends[c].at[j], recvs[c].at[j], behind(offset))

    sub16 = lax.broadcasted_iota(jnp.int32, (16, HD), 0)
    column = lax.broadcasted_iota(jnp.int32, (16, 1), 0)
    position = lax.broadcasted_iota(jnp.int32, (16, BLK), 1)
    stats = jnp.zeros((8, HD), F32)

    for c, (start, count, rows) in enumerate(CHUNKS):
        wait_bytes(recvs[c].at[others], recv_sem.at[1 + c])
        total = sends[c][PEERS]
        for j in range(PEERS):
            total = total + recvs[c][j]
        total = total.astype(BF16).astype(F32)
        per_tile = 8 // count
        for entry in range(ENTRIES):
            row = entry * count
            query_rows[pl.ds(16 * start + entry, count, stride=16), :] = total[row : row + count]

        for pair in range(start // 2, (start + count) // 2):
            a, b = 2 * pair, 2 * pair + 1
            k_loads[pair].wait()
            v_loads[pair].wait()
            queries = jnp.concatenate(
                [query_rows[16 * a : 16 * a + 8, :], query_rows[16 * b : 16 * b + 8, :]], axis=0
            )
            new_keys = jnp.where(
                sub16 < 8, query_rows[16 * a + 8 : 16 * a + 9, :], query_rows[16 * b + 8 : 16 * b + 9, :]
            )
            new_values = jnp.where(
                sub16 < 8, query_rows[16 * a + 9 : 16 * a + 10, :], query_rows[16 * b + 9 : 16 * b + 10, :]
            )
            left = jnp.concatenate(
                [jnp.where(sub16 < 8, queries, 0.0), jnp.where(sub16 < 8, 0.0, queries)], axis=1
            ).astype(BF16)
            keys = jnp.concatenate([k_v[a], k_v[b]], axis=1)
            scores = lax.dot_general(left, keys, NT, preferred_element_type=F32) * SCALE
            limit_a = lengths[jnp.maximum(table[0, a], 0)] - BLK * table[1, a]
            limit_b = lengths[jnp.maximum(table[0, b], 0)] - BLK * table[1, b]
            limit = jnp.where(column < 8, limit_a, limit_b)
            scores = jnp.where(position < limit, scores, FLOOR)
            top = jnp.max(scores, axis=1, keepdims=True)
            weights = jnp.exp(scores - top)
            block_total = jnp.sum(weights, axis=1, keepdims=True)
            is_first = jnp.where(column < 8, table[1, a], table[1, b]) == 0
            own = jnp.sum(queries * new_keys, axis=1, keepdims=True) * SCALE
            own = jnp.where(is_first, own, FLOOR)
            highest = jnp.maximum(top, own)
            factor = jnp.exp(top - highest)
            own_weight = jnp.where(is_first, jnp.exp(own - highest), 0.0)
            slot_total = block_total * factor + own_weight
            for s, part in ((a, slice(0, 8)), (b, slice(8, 16))):
                stats = jnp.where(lane == s, highest[part], stats)
                stats = jnp.where(lane == 16 + s, slot_total[part], stats)
            if b == SLOTS - 1:
                stats_all[PEERS] = stats
                for j, offset in enumerate(OFFSETS):
                    send(7, stats_all.at[PEERS], stats_all.at[j], ahead(offset))
            values = jnp.concatenate([v_v[a], v_v[b]], axis=1)
            both = jnp.dot(weights.astype(BF16), values, preferred_element_type=F32)
            block_out = jnp.where(sub16 < 8, both[:, :HD], both[:, HD:])
            slot_out = (block_out * factor + own_weight * new_values) / slot_total
            outs_all[PEERS, 16 * pair : 16 * pair + 16, :] = slot_out.astype(BF16)
        part = pl.ds(8 * start, 8 * count)
        for j, offset in enumerate(OFFSETS):
            send(4 + c, outs_all.at[PEERS, part], outs_all.at[j, part], ahead(offset))

    def side_by_side(tiles, shift):
        near = jnp.full((8, HD), -1.0, F32)
        far = jnp.full((8, HD), -1.0, F32)
        for j in range(KV):
            at = SLOTS * j
            moved = pltpu.roll(tiles(j), (at - shift) % HD, 1)
            if at < HD:
                near = jnp.where((lane >= at) & (lane < at + SLOTS), moved, near)
            if at + SLOTS > HD:
                far = jnp.where((lane >= at - HD) & (lane < at + SLOTS - HD), moved, far)
        return jnp.concatenate([near, far], axis=1)

    owners = side_by_side(lambda j: first_all[j], OWNER_LANE)
    belongs = lax.broadcasted_iota(jnp.int32, (ROWS, 2 * HD), 0).astype(F32) == owners[0:1]

    wait_bytes(stats_all.at[others], recv_sem.at[7])
    tops = side_by_side(lambda j: stats_all[j], 0)
    totals = side_by_side(lambda j: stats_all[j], 16)
    shares = []
    for g in range(G):
        masked = jnp.where(belongs, tops[g : g + 1], -3e38)
        highest = jnp.max(masked, axis=1, keepdims=True)
        share = jnp.where(belongs, jnp.exp(masked - highest) * totals[g : g + 1], 0.0)
        share = share / jnp.sum(share, axis=1, keepdims=True)
        upper = share.astype(BF16)
        lower = (share - upper.astype(F32)).astype(BF16)
        shares.append(jnp.concatenate([upper, lower], axis=0))

    for c, (start, count, rows) in enumerate(CHUNKS):
        wait_bytes(outs_all.at[others, pl.ds(8 * start, 8 * count)], recv_sem.at[4 + c])
    outs_wide[...] = outs_all[...].astype(F32).reshape(KV * SLOTS * G, HD)
    attended = []
    for g in range(G):
        slots = outs_wide[pl.ds(g, KV * SLOTS, stride=G), :].astype(BF16)
        slots = jnp.concatenate([slots, jnp.zeros((2 * HD - KV * SLOTS, HD), BF16)], axis=0)
        both = jnp.dot(shares[g], slots, preferred_element_type=F32)
        attended.append((both[:ROWS] + both[ROWS:]).astype(BF16))
    attended = jnp.concatenate(attended, axis=1)

    loads[3].wait()
    mine = pl.ds(pl.multiple_of(core * HALF, HALF), HALF)
    theirs = pl.ds(pl.multiple_of((1 - core) * HALF, HALF), HALF)
    half_send[...] = jnp.dot(attended, w_out[:, theirs], preferred_element_type=F32)
    send(8, half_send, half_recv, sibling)
    own_half = jnp.dot(attended, w_out[:, mine], preferred_element_type=F32)
    wait_bytes(half_recv, recv_sem.at[8])
    z_all[my_z] = (own_half + half_recv[...]).astype(BF16)
    for peer in z_peers:
        send(9, z_all.at[my_z], z_all.at[my_z], peer)
    wait_bytes(z_all.at[pl.ds(0, SIDE - 1)], recv_sem.at[9])
    parts = [z_all[z].astype(F32) for z in range(SIDE)]
    done = (((parts[0] + parts[1]) + parts[2]) + parts[3]).astype(BF16)
    done_send[...] = done
    send(10, done_send, done_recv, sibling)
    out_ref[:, mine] = done
    wait_bytes(done_recv, recv_sem.at[10])
    out_ref[:, theirs] = done_recv[...]

    wait_bytes(first_all.at[others], send_sem.at[0])
    for c, (start, count, rows) in enumerate(CHUNKS):
        wait_bytes(sends[c].at[others], send_sem.at[1 + c])
        wait_bytes(outs_all.at[others, pl.ds(8 * start, 8 * count)], send_sem.at[4 + c])
    wait_bytes(stats_all.at[others], send_sem.at[7])
    wait_bytes(half_send, send_sem.at[8])
    wait_bytes(z_all.at[pl.ds(0, SIDE - 1)], send_sem.at[9])
    wait_bytes(done_send, send_sem.at[10])


def per_device(tokens, gain, w_qkv, w_out, k_cache, v_cache, lengths, block_table):
    features = tokens.shape[1]
    anywhere = pl.BlockSpec(memory_space=pl.ANY)
    return pl.pallas_call(
        kernel,
        out_shape=jax.ShapeDtypeStruct((ROWS, features), BF16),
        in_specs=[anywhere] * 8,
        out_specs=pl.BlockSpec(memory_space=pltpu.VMEM),
        scratch_shapes=[
            pltpu.VMEM((ROWS, features), BF16),
            pltpu.VMEM((1, features), F32),
            pltpu.VMEM((features, ENTRIES * HD), BF16),
            pltpu.VMEM((G * HD, features), BF16),
            pltpu.VMEM((SLOTS, BLK, HD), BF16),
            pltpu.VMEM((SLOTS, BLK, HD), BF16),
            pltpu.VMEM((KV, 8, HD), F32),
        ]
        + [pltpu.VMEM((KV, rows, HD), F32) for _, _, rows in CHUNKS]
        + [pltpu.VMEM((PEERS, rows, HD), F32) for _, _, rows in CHUNKS]
        + [
            pltpu.VMEM((SLOTS * 16, HD), F32),
            pltpu.VMEM((KV, SLOTS * G, HD), BF16),
            pltpu.VMEM((KV, 8, HD), F32),
            pltpu.VMEM((KV * SLOTS * G, HD), F32),
            pltpu.VMEM((ROWS, HALF), F32),
            pltpu.VMEM((ROWS, HALF), F32),
            pltpu.VMEM((SIDE, ROWS, HALF), BF16),
            pltpu.VMEM((ROWS, HALF), BF16),
            pltpu.VMEM((ROWS, HALF), BF16),
            pltpu.SMEM((ROWS,), jnp.int32),
            pltpu.SMEM((2, SLOTS), jnp.int32),
            pltpu.SemaphoreType.DMA((6,)),
            pltpu.SemaphoreType.DMA((2, SLOTS // 2)),
            pltpu.SemaphoreType.DMA((11,)),
            pltpu.SemaphoreType.DMA((11,)),
        ],
        compiler_params=pltpu.CompilerParams(
            collective_id=0, has_side_effects=True, vmem_limit_bytes=56 << 20
        ),
    )(
        tokens,
        gain.reshape(1, features),
        w_qkv.reshape(features, ENTRIES * HD),
        w_out.reshape(G * HD, features),
        k_cache.reshape(SLOTS, BLK, HD),
        v_cache.reshape(SLOTS, BLK, HD),
        lengths,
        block_table.T,
    )


def solution(mesh):
    placed = (
        P(None, "kv"),
        P("kv"),
        P("kv", "tp", None),
        P("tp", None, "kv"),
        P("tp", "kv", None, None),
        P("tp", "kv", None, None),
        P(),
        P("kv", None),
    )
    return jax.shard_map(
        per_device, mesh=mesh, in_specs=placed, out_specs=P(None, "kv"), check_vma=False
    )
```

```python
import functools

import jax
import jax.numpy as jnp
from jax import lax
from jax.experimental import pallas as pl
from jax.experimental.pallas import tpu as pltpu
from jax.sharding import PartitionSpec as P

D = 8192
HD = 128
G = 8
ROWS = 64
SLOTS = 10
ENTRIES = G + 2
BLK = 4096
SIDE = 4
KV = SIDE * SIDE
PEERS = KV - 1
HALF = 256

EPSILON = 1e-05
FLOOR = -1e30
SCALE = HD ** (-0.5)

MESH = pl.DeviceIdType.MESH
F32 = jnp.float32
BF16 = jnp.bfloat16

SQUARE_LANE = 8
OWNER_LANE = 16

EARLY_VALUES = 1
EARLY_KEYS = 3
TURN = 512

CHUNKS = ((0, 2, 32), (2, 4, 48), (6, 4, 48))
LANES = (128, 0, 64)

STEPS = 32000.0


def ring_distance(step):
    return min(step, SIDE - step)


OFFSETS = sorted(
    [(a, b) for a in range(SIDE) for b in range(SIDE) if (a, b) != (0, 0)],
    key=lambda m: -(ring_distance(m[0]) + ring_distance(m[1])),
)


def wait_bytes(ref, sem):
    pltpu.make_async_copy(ref, ref, sem).wait()


def kernel(
    tokens_hbm,
    gain_hbm,
    w_qkv_hbm,
    w_out_hbm,
    k_hbm,
    v_hbm,
    lengths_hbm,
    table_hbm,
    out_ref,
    tokens_v,
    gain_v,
    w_qkv,
    w_out,
    k_v,
    k_turned,
    v_v,
    first_all,
    send0,
    send1,
    send2,
    recv0,
    recv1,
    recv2,
    query_rows,
    outs0,
    outs1,
    outs2,
    stats_all,
    wide0,
    wide1,
    wide2,
    half_send,
    half_recv,
    z_all,
    done_send,
    lengths,
    table,
    load_sem,
    kv_sem,
    send_sem,
    recv_sem,
):
    me = lax.axis_index("kv")
    my_x, my_y = me // SIDE, me % SIDE
    tp = lax.axis_index("tp")
    my_z, core = tp // 2, tp % 2

    def ahead(offset):
        return {"kv": ((my_x + offset[0]) % SIDE) * SIDE + (my_y + offset[1]) % SIDE}

    def behind(offset):
        return ahead(((SIDE - offset[0]) % SIDE, (SIDE - offset[1]) % SIDE))

    sibling = {"tp": my_z * 2 + (1 - core)}
    z_peers = [{"tp": ((my_z + step) % SIDE) * 2 + core} for step in (2, 1, 3)]

    barrier = pltpu.get_barrier_semaphore()
    for offset in OFFSETS:
        pl.semaphore_signal(barrier, inc=1, device_id=ahead(offset), device_id_type=MESH)
    for peer in z_peers + [sibling]:
        pl.semaphore_signal(barrier, inc=1, device_id=peer, device_id_type=MESH)

    loads = [
        pltpu.make_async_copy(tokens_hbm, tokens_v, load_sem.at[0]),
        pltpu.make_async_copy(gain_hbm, gain_v, load_sem.at[1]),
        pltpu.make_async_copy(w_qkv_hbm, w_qkv, load_sem.at[2]),
        pltpu.make_async_copy(w_out_hbm, w_out, load_sem.at[3]),
        pltpu.make_async_copy(table_hbm, table, load_sem.at[4]),
        pltpu.make_async_copy(lengths_hbm, lengths, load_sem.at[5]),
    ]
    k_loads, v_loads = [], []
    for pair in range(SLOTS // 2):
        part = pl.ds(2 * pair, 2)
        k_loads.append(pltpu.make_async_copy(k_hbm.at[part], k_v.at[part], kv_sem.at[0, pair]))
        v_loads.append(pltpu.make_async_copy(v_hbm.at[part], v_v.at[part], kv_sem.at[1, pair]))
    for load in loads[:3] + loads[4:]:
        load.start()
    for pair in range(SLOTS // 2):
        k_loads[pair].start()
    for pair in range(EARLY_VALUES):
        v_loads[pair].start()

    sub = lax.broadcasted_iota(jnp.int32, (8, HD), 0)
    lane = lax.broadcasted_iota(jnp.int32, (8, HD), 1)

    loads[0].wait()
    tokens = tokens_v[...].astype(F32)
    squares = jnp.sum(tokens * tokens, axis=1, keepdims=True)
    loads[4].wait()
    loads[5].wait()
    owners = jnp.full((8, HD), -1, jnp.int32)
    for slot in range(SLOTS):
        owners = jnp.where(lane == OWNER_LANE + slot, table[0, slot], owners)
    for c, (start, count, _) in enumerate(CHUNKS):
        for s in range(count):
            owners = jnp.where((lane == c) & (sub % count == s), table[0, start + s], owners)
    tile = owners.astype(F32)
    for k in range(ROWS // 8):
        tile = jnp.where(lane == SQUARE_LANE + k, squares[8 * k : 8 * k + 8], tile)
    first_all[PEERS] = tile

    pl.semaphore_wait(barrier, PEERS + 4)

    def send(phase, src, dst, peer):
        pltpu.make_async_remote_copy(
            src_ref=src,
            dst_ref=dst,
            send_sem=send_sem.at[phase],
            recv_sem=recv_sem.at[phase],
            device_id=peer,
            device_id_type=MESH,
        ).start()

    others = pl.ds(0, PEERS)

    for j, offset in enumerate(OFFSETS):
        send(0, first_all.at[PEERS], first_all.at[j], ahead(offset))

    def turn_keys(pair):
        k_loads[pair].wait()
        for half in range(2):
            for at in range(0, BLK, TURN):
                k_turned[pair, HD * half : HD * half + HD, at : at + TURN] = k_v[
                    2 * pair + half, at : at + TURN
                ].T

    for pair in range(EARLY_KEYS):
        turn_keys(pair)
    loads[1].wait()
    loads[2].wait()
    wait_bytes(first_all.at[others], recv_sem.at[0])

    for pair in range(EARLY_VALUES, SLOTS // 2):
        v_loads[pair].start()
    loads[3].start()
    squares = first_all[0]
    for j in range(1, KV):
        squares = squares + first_all[j]
    inverse = lax.rsqrt(squares / D + EPSILON)
    gains = gain_v[...]
    normed = jnp.concatenate(
        [tokens[8 * k : 8 * k + 8] * inverse[:, SQUARE_LANE + k : SQUARE_LANE + k + 1] * gains for k in range(ROWS // 8)], axis=0
    ).astype(BF16)
    partial = jnp.dot(normed, w_qkv[...], preferred_element_type=F32)
    largest = jnp.max(jnp.abs(partial), axis=1, keepdims=True)
    exponent = jnp.ceil(jnp.log2(jnp.maximum(largest, 1e-30)))
    whole = jnp.round(partial * (STEPS * jnp.exp2(-exponent)))
    coarse = jnp.floor(whole * (1.0 / 256.0))
    fine = whole - 256.0 * coarse
    exponents = jnp.broadcast_to(exponent, (ROWS, HD))
    stacked = jnp.concatenate(
        [
            jnp.concatenate([coarse, jnp.zeros_like(exponents)], axis=1),
            jnp.concatenate([fine, exponents], axis=1),
        ],
        axis=0,
    ).astype(BF16)

    row_of_lane = lax.broadcasted_iota(jnp.int32, (KV * 8, HD), 1)
    row_number = (row_of_lane % ROWS).astype(F32)
    part_weight = jnp.where(row_of_lane < ROWS, 256.0, 1.0)
    everyone = first_all[...].reshape(KV * 8, HD)
    sub3 = lax.broadcasted_iota(jnp.int32, (KV, 8, HD), 1)
    sends = (send0, send1, send2)
    recvs = (recv0, recv1, recv2)
    outs = (outs0, outs1, outs2)
    wides = (wide0, wide1, wide2)
    for c, (start, count, rows) in enumerate(CHUNKS):
        pick = jnp.where(everyone[:, c : c + 1] == row_number, part_weight, 0.0).astype(BF16)
        packed = jnp.dot(pick, stacked, preferred_element_type=F32).reshape(KV, 8, (ENTRIES + 1) * HD)
        per_tile = 8 // count
        tiles = []
        for k in range(rows // 8 - 1):
            tile = packed[:, :, per_tile * k * HD : (per_tile * k + 1) * HD]
            for e in range(1, per_tile):
                entry = per_tile * k + e
                if entry < ENTRIES:
                    tile = jnp.where(
                        sub3 >= e * count, packed[:, :, entry * HD : (entry + 1) * HD], tile
                    )
            tiles.append(tile)
        tiles.append(packed[:, :, ENTRIES * HD :])
        sends[c][...] = jnp.concatenate(tiles, axis=1).astype(jnp.int32).astype(jnp.int16)
        for j, offset in enumerate(OFFSETS):
            send(1 + c, sends[c].at[j], recvs[c].at[j], behind(offset))

    for pair in range(EARLY_KEYS, SLOTS // 2):
        turn_keys(pair)

    sub16 = lax.broadcasted_iota(jnp.int32, (16, HD), 0)
    column = lax.broadcasted_iota(jnp.int32, (16, 1), 0)
    position = lax.broadcasted_iota(jnp.int32, (16, BLK), 1)
    stats = jnp.zeros((8, HD), F32)

    for c, (start, count, rows) in enumerate(CHUNKS):
        wait_bytes(recvs[c].at[others], recv_sem.at[1 + c])
        total = 0.0
        for j in range(KV):
            got = (sends[c][PEERS] if j == PEERS else recvs[c][j]).astype(jnp.int32).astype(F32)
            got = got.reshape(rows // 8, 8, HD)
            total = total + got[:-1] * (jnp.exp2(got[-1:]) * (1.0 / STEPS))
        total = total.reshape(rows - 8, HD)
        total = total.astype(BF16).astype(F32)
        per_tile = 8 // count
        for entry in range(ENTRIES):
            row = entry * count
            query_rows[pl.ds(16 * start + entry, count, stride=16), :] = total[row : row + count]

        for pair in range(start // 2, (start + count) // 2):
            a, b = 2 * pair, 2 * pair + 1
            v_loads[pair].wait()
            queries = jnp.concatenate(
                [query_rows[16 * a : 16 * a + 8, :], query_rows[16 * b : 16 * b + 8, :]], axis=0
            )
            new_keys = jnp.where(
                sub16 < 8, query_rows[16 * a + 8 : 16 * a + 9, :], query_rows[16 * b + 8 : 16 * b + 9, :]
            )
            new_values = jnp.where(
                sub16 < 8, query_rows[16 * a + 9 : 16 * a + 10, :], query_rows[16 * b + 9 : 16 * b + 10, :]
            )
            left = jnp.concatenate(
                [jnp.where(sub16 < 8, queries, 0.0), jnp.where(sub16 < 8, 0.0, queries)], axis=1
            ).astype(BF16)
            scores = jnp.dot(left, k_turned[pair], preferred_element_type=F32) * SCALE
            limit_a = lengths[jnp.maximum(table[0, a], 0)] - BLK * table[1, a]
            limit_b = lengths[jnp.maximum(table[0, b], 0)] - BLK * table[1, b]
            limit = jnp.where(column < 8, limit_a, limit_b)
            scores = jnp.where(position < limit, scores, FLOOR)
            top = jnp.max(scores, axis=1, keepdims=True)
            weights = jnp.exp(scores - top)
            block_total = jnp.sum(weights, axis=1, keepdims=True)
            is_first = jnp.where(column < 8, table[1, a], table[1, b]) == 0
            own = jnp.sum(queries * new_keys, axis=1, keepdims=True) * SCALE
            own = jnp.where(is_first, own, FLOOR)
            highest = jnp.maximum(top, own)
            factor = jnp.exp(top - highest)
            own_weight = jnp.where(is_first, jnp.exp(own - highest), 0.0)
            slot_total = block_total * factor + own_weight
            for s, part in ((a, slice(0, 8)), (b, slice(8, 16))):
                stats = jnp.where(lane == s, highest[part], stats)
                stats = jnp.where(lane == 16 + s, slot_total[part], stats)
            if b == SLOTS - 1:
                stats_all[PEERS] = stats
                for j, offset in enumerate(OFFSETS):
                    send(7, stats_all.at[PEERS], stats_all.at[j], ahead(offset))
            values = jnp.concatenate([v_v[a], v_v[b]], axis=1)
            both = jnp.dot(weights.astype(BF16), values, preferred_element_type=F32)
            block_out = jnp.where(sub16 < 8, both[:, :HD], both[:, HD:])
            slot_out = (block_out * factor + own_weight * new_values) / slot_total
            at = 8 * (a - start)
            outs[c][PEERS, at : at + 16, :] = slot_out.astype(BF16)
        for j, offset in enumerate(OFFSETS):
            send(4 + c, outs[c].at[PEERS], outs[c].at[j], ahead(offset))

    def side_by_side(tiles, shift):
        halves = [jnp.full((8, HD), -1.0, F32), jnp.full((8, HD), -1.0, F32)]
        for (start, count, _), first in zip(CHUNKS, LANES):
            for j in range(KV):
                half, at = divmod(first + count * j, HD)
                moved = pltpu.roll(tiles(j), (at - start - shift) % HD, 1)
                halves[half] = jnp.where((lane >= at) & (lane < at + count), moved, halves[half])
        return jnp.concatenate(halves, axis=1)

    owners = side_by_side(lambda j: first_all[j], OWNER_LANE)
    belongs = lax.broadcasted_iota(jnp.int32, (ROWS, 2 * HD), 0).astype(F32) == owners[0:1]

    wait_bytes(stats_all.at[others], recv_sem.at[7])
    tops = side_by_side(lambda j: stats_all[j], 0)
    totals = side_by_side(lambda j: stats_all[j], 16)
    shares = []
    for g in range(G):
        masked = jnp.where(belongs, tops[g : g + 1], -3e38)
        highest = jnp.max(masked, axis=1, keepdims=True)
        share = jnp.where(belongs, jnp.exp(masked - highest) * totals[g : g + 1], 0.0)
        share = share / jnp.sum(share, axis=1, keepdims=True)
        upper = share.astype(BF16)
        lower = (share - upper.astype(F32)).astype(BF16)
        shares.append(jnp.concatenate([upper, lower], axis=0))

    def arrived(c):
        wait_bytes(outs[c].at[others], recv_sem.at[4 + c])
        wides[c][...] = outs[c][...].astype(F32).reshape(wides[c].shape)

    def slots_of(c, g):
        return wides[c][pl.ds(g, wides[c].shape[0] // G, stride=G), :].astype(BF16)

    for c in range(len(CHUNKS)):
        arrived(c)
    attended = []
    for g in range(G):
        slots = [slots_of(c, g) for c in sorted(range(len(CHUNKS)), key=lambda c: LANES[c])]
        slots = jnp.concatenate(slots + [jnp.zeros((2 * HD - KV * SLOTS, HD), BF16)], axis=0)
        both = jnp.dot(shares[g], slots, preferred_element_type=F32)
        attended.append((both[:ROWS] + both[ROWS:]).astype(BF16))
    attended = jnp.concatenate(attended, axis=1)

    loads[3].wait()
    mine = pl.ds(pl.multiple_of(core * HALF, HALF), HALF)
    theirs = pl.ds(pl.multiple_of((1 - core) * HALF, HALF), HALF)
    half_send[...] = jnp.dot(attended, w_out[:, theirs], preferred_element_type=F32)
    send(8, half_send, half_recv, sibling)
    own_half = jnp.dot(attended, w_out[:, mine], preferred_element_type=F32)
    wait_bytes(half_recv, recv_sem.at[8])
    z_all[my_z] = (own_half + half_recv[...]).astype(BF16)
    for peer in z_peers:
        send(9, z_all.at[my_z], z_all.at[my_z], peer)
    wait_bytes(z_all.at[pl.ds(0, SIDE - 1)], recv_sem.at[9])
    parts = [z_all[z].astype(F32) for z in range(SIDE)]
    done = (((parts[0] + parts[1]) + parts[2]) + parts[3]).astype(BF16)
    done_send[...] = done
    send(10, done_send, out_ref.at[:, mine], sibling)
    keep = pltpu.make_async_copy(done_send, out_ref.at[:, mine], load_sem.at[6])
    keep.start()

    wait_bytes(first_all.at[others], send_sem.at[0])
    for c, (start, count, rows) in enumerate(CHUNKS):
        wait_bytes(sends[c].at[others], send_sem.at[1 + c])
        wait_bytes(outs[c].at[others], send_sem.at[4 + c])
    wait_bytes(stats_all.at[others], send_sem.at[7])
    wait_bytes(half_send, send_sem.at[8])
    wait_bytes(z_all.at[pl.ds(0, SIDE - 1)], send_sem.at[9])
    wait_bytes(done_send, send_sem.at[10])
    wait_bytes(out_ref.at[:, theirs], recv_sem.at[10])
    keep.wait()


def per_device(tokens, gain, w_qkv, w_out, k_cache, v_cache, lengths, block_table):
    features = tokens.shape[1]
    anywhere = pl.BlockSpec(memory_space=pl.ANY)
    return pl.pallas_call(
        kernel,
        out_shape=jax.ShapeDtypeStruct((ROWS, features), BF16),
        in_specs=[anywhere] * 8,
        out_specs=anywhere,
        scratch_shapes=[
            pltpu.VMEM((ROWS, features), BF16),
            pltpu.VMEM((1, features), F32),
            pltpu.VMEM((features, ENTRIES * HD), BF16),
            pltpu.VMEM((G * HD, features), BF16),
            pltpu.VMEM((SLOTS, BLK, HD), BF16),
            pltpu.VMEM((SLOTS // 2, 2 * HD, BLK), BF16),
            pltpu.VMEM((SLOTS, BLK, HD), BF16),
            pltpu.VMEM((KV, 8, HD), F32),
        ]
        + [pltpu.VMEM((KV, rows, HD), jnp.int16) for _, _, rows in CHUNKS]
        + [pltpu.VMEM((PEERS, rows, HD), jnp.int16) for _, _, rows in CHUNKS]
        + [
            pltpu.VMEM((SLOTS * 16, HD), F32),
        ]
        + [pltpu.VMEM((KV, count * G, HD), BF16) for _, count, _ in CHUNKS]
        + [pltpu.VMEM((KV, 8, HD), F32)]
        + [pltpu.VMEM((KV * count * G, HD), F32) for _, count, _ in CHUNKS]
        + [
            pltpu.VMEM((ROWS, HALF), F32),
            pltpu.VMEM((ROWS, HALF), F32),
            pltpu.VMEM((SIDE, ROWS, HALF), BF16),
            pltpu.VMEM((ROWS, HALF), BF16),
            pltpu.SMEM((ROWS,), jnp.int32),
            pltpu.SMEM((2, SLOTS), jnp.int32),
            pltpu.SemaphoreType.DMA((7,)),
            pltpu.SemaphoreType.DMA((2, SLOTS // 2)),
            pltpu.SemaphoreType.DMA((11,)),
            pltpu.SemaphoreType.DMA((11,)),
        ],
        compiler_params=pltpu.CompilerParams(
            collective_id=0, has_side_effects=True, vmem_limit_bytes=56 << 20
        ),
    )(
        tokens,
        gain.reshape(1, features),
        w_qkv.reshape(features, ENTRIES * HD),
        w_out.reshape(G * HD, features),
        k_cache.reshape(SLOTS, BLK, HD),
        v_cache.reshape(SLOTS, BLK, HD),
        lengths,
        block_table.T,
    )


def solution(mesh):
    placed = (
        P(None, "kv"),
        P("kv"),
        P("kv", "tp", None),
        P("tp", None, "kv"),
        P("tp", "kv", None, None),
        P("tp", "kv", None, None),
        P(),
        P("kv", None),
    )
    return jax.shard_map(
        per_device, mesh=mesh, in_specs=placed, out_specs=P(None, "kv"), check_vma=False
    )
```

```python
import functools

import jax
import jax.numpy as jnp
from jax import lax
from jax.experimental import pallas as pl
from jax.experimental.pallas import tpu as pltpu
from jax.sharding import PartitionSpec as P

D = 8192
HD = 128
G = 8
ROWS = 64
SLOTS = 10
ENTRIES = G + 2
BLK = 4096
SIDE = 4
KV = SIDE * SIDE
PEERS = KV - 1
HALF = 256

EPSILON = 1e-05
FLOOR = -1e30
SCALE = HD ** (-0.5)

MESH = pl.DeviceIdType.MESH
F32 = jnp.float32
BF16 = jnp.bfloat16

SQUARE_LANE = 8
OWNER_LANE = 16

EARLY_VALUES = 1
EARLY_KEYS = 3
TURN = 512

CHUNKS = ((0, 4, 48), (4, 4, 48), (8, 2, 32))
LANES = (0, 64, 128)

STEPS = 32000.0


def ring_distance(step):
    return min(step, SIDE - step)


OFFSETS = sorted(
    [(a, b) for a in range(SIDE) for b in range(SIDE) if (a, b) != (0, 0)],
    key=lambda m: -(ring_distance(m[0]) + ring_distance(m[1])),
)


def wait_bytes(ref, sem):
    pltpu.make_async_copy(ref, ref, sem).wait()


def kernel(
    tokens_hbm,
    gain_hbm,
    w_qkv_hbm,
    w_out_hbm,
    k_hbm,
    v_hbm,
    lengths_hbm,
    table_hbm,
    out_ref,
    tokens_v,
    gain_v,
    w_qkv,
    w_out,
    k_v,
    k_turned,
    v_v,
    first_all,
    send0,
    send1,
    send2,
    recv0,
    recv1,
    recv2,
    query_rows,
    outs0,
    outs1,
    outs2,
    stats_all,
    wide0,
    wide1,
    wide2,
    half_send,
    half_recv,
    z_all,
    done_send,
    lengths,
    table,
    load_sem,
    kv_sem,
    send_sem,
    recv_sem,
):
    me = lax.axis_index("kv")
    my_x, my_y = me // SIDE, me % SIDE
    tp = lax.axis_index("tp")
    my_z, core = tp // 2, tp % 2

    def ahead(offset):
        return {"kv": ((my_x + offset[0]) % SIDE) * SIDE + (my_y + offset[1]) % SIDE}

    def behind(offset):
        return ahead(((SIDE - offset[0]) % SIDE, (SIDE - offset[1]) % SIDE))

    sibling = {"tp": my_z * 2 + (1 - core)}
    z_peers = [{"tp": ((my_z + step) % SIDE) * 2 + core} for step in (2, 1, 3)]

    barrier = pltpu.get_barrier_semaphore()
    for offset in OFFSETS:
        pl.semaphore_signal(barrier, inc=1, device_id=ahead(offset), device_id_type=MESH)
    for peer in z_peers + [sibling]:
        pl.semaphore_signal(barrier, inc=1, device_id=peer, device_id_type=MESH)

    loads = [
        pltpu.make_async_copy(tokens_hbm, tokens_v, load_sem.at[0]),
        pltpu.make_async_copy(gain_hbm, gain_v, load_sem.at[1]),
        pltpu.make_async_copy(w_qkv_hbm, w_qkv, load_sem.at[2]),
        pltpu.make_async_copy(w_out_hbm, w_out, load_sem.at[3]),
        pltpu.make_async_copy(table_hbm, table, load_sem.at[4]),
        pltpu.make_async_copy(lengths_hbm, lengths, load_sem.at[5]),
    ]
    k_loads, v_loads = [], []
    for pair in range(SLOTS // 2):
        part = pl.ds(2 * pair, 2)
        k_loads.append(pltpu.make_async_copy(k_hbm.at[part], k_v.at[part], kv_sem.at[0, pair]))
        v_loads.append(pltpu.make_async_copy(v_hbm.at[part], v_v.at[part], kv_sem.at[1, pair]))
    for load in loads[:3] + loads[4:]:
        load.start()
    for pair in range(SLOTS // 2):
        k_loads[pair].start()
    for pair in range(EARLY_VALUES):
        v_loads[pair].start()

    sub = lax.broadcasted_iota(jnp.int32, (8, HD), 0)
    lane = lax.broadcasted_iota(jnp.int32, (8, HD), 1)

    loads[0].wait()
    tokens = tokens_v[...].astype(F32)
    squares = jnp.sum(tokens * tokens, axis=1, keepdims=True)
    loads[4].wait()
    loads[5].wait()
    owners = jnp.full((8, HD), -1, jnp.int32)
    for slot in range(SLOTS):
        owners = jnp.where(lane == OWNER_LANE + slot, table[0, slot], owners)
    for c, (start, count, _) in enumerate(CHUNKS):
        for s in range(count):
            owners = jnp.where((lane == c) & (sub % count == s), table[0, start + s], owners)
    tile = owners.astype(F32)
    for k in range(ROWS // 8):
        tile = jnp.where(lane == SQUARE_LANE + k, squares[8 * k : 8 * k + 8], tile)
    first_all[PEERS] = tile

    pl.semaphore_wait(barrier, PEERS + 4)

    def send(phase, src, dst, peer):
        pltpu.make_async_remote_copy(
            src_ref=src,
            dst_ref=dst,
            send_sem=send_sem.at[phase],
            recv_sem=recv_sem.at[phase],
            device_id=peer,
            device_id_type=MESH,
        ).start()

    others = pl.ds(0, PEERS)

    for j, offset in enumerate(OFFSETS):
        send(0, first_all.at[PEERS], first_all.at[j], ahead(offset))

    def turn_keys(pair):
        k_loads[pair].wait()
        for half in range(2):
            for at in range(0, BLK, TURN):
                k_turned[pair, HD * half : HD * half + HD, at : at + TURN] = k_v[
                    2 * pair + half, at : at + TURN
                ].T

    for pair in range(EARLY_KEYS):
        turn_keys(pair)
    loads[1].wait()
    loads[2].wait()
    wait_bytes(first_all.at[others], recv_sem.at[0])

    for pair in range(EARLY_VALUES, SLOTS // 2):
        v_loads[pair].start()
    loads[3].start()
    squares = first_all[0]
    for j in range(1, KV):
        squares = squares + first_all[j]
    inverse = lax.rsqrt(squares / D + EPSILON)
    gains = gain_v[...]
    normed = jnp.concatenate(
        [tokens[8 * k : 8 * k + 8] * inverse[:, SQUARE_LANE + k : SQUARE_LANE + k + 1] * gains for k in range(ROWS // 8)], axis=0
    ).astype(BF16)
    partial = jnp.dot(normed, w_qkv[...], preferred_element_type=F32)
    largest = jnp.max(jnp.abs(partial), axis=1, keepdims=True)
    exponent = jnp.ceil(jnp.log2(jnp.maximum(largest, 1e-30)))
    whole = jnp.round(partial * (STEPS * jnp.exp2(-exponent)))
    coarse = jnp.floor(whole * (1.0 / 256.0))
    fine = whole - 256.0 * coarse
    exponents = jnp.broadcast_to(exponent, (ROWS, HD))
    stacked = jnp.concatenate(
        [
            jnp.concatenate([coarse, jnp.zeros_like(exponents)], axis=1),
            jnp.concatenate([fine, exponents], axis=1),
        ],
        axis=0,
    ).astype(BF16)

    row_of_lane = lax.broadcasted_iota(jnp.int32, (KV * 8, HD), 1)
    row_number = (row_of_lane % ROWS).astype(F32)
    part_weight = jnp.where(row_of_lane < ROWS, 256.0, 1.0)
    everyone = first_all[...].reshape(KV * 8, HD)
    sub3 = lax.broadcasted_iota(jnp.int32, (KV, 8, HD), 1)
    sends = (send0, send1, send2)
    recvs = (recv0, recv1, recv2)
    outs = (outs0, outs1, outs2)
    wides = (wide0, wide1, wide2)
    for c, (start, count, rows) in enumerate(CHUNKS):
        pick = jnp.where(everyone[:, c : c + 1] == row_number, part_weight, 0.0).astype(BF16)
        packed = jnp.dot(pick, stacked, preferred_element_type=F32).reshape(KV, 8, (ENTRIES + 1) * HD)
        per_tile = 8 // count
        tiles = []
        for k in range(rows // 8 - 1):
            tile = packed[:, :, per_tile * k * HD : (per_tile * k + 1) * HD]
            for e in range(1, per_tile):
                entry = per_tile * k + e
                if entry < ENTRIES:
                    tile = jnp.where(
                        sub3 >= e * count, packed[:, :, entry * HD : (entry + 1) * HD], tile
                    )
            tiles.append(tile)
        tiles.append(packed[:, :, ENTRIES * HD :])
        sends[c][...] = jnp.concatenate(tiles, axis=1).astype(jnp.int32).astype(jnp.int16)
        for j, offset in enumerate(OFFSETS):
            send(1 + c, sends[c].at[j], recvs[c].at[j], behind(offset))

    for pair in range(EARLY_KEYS, SLOTS // 2):
        turn_keys(pair)

    sub16 = lax.broadcasted_iota(jnp.int32, (16, HD), 0)
    column = lax.broadcasted_iota(jnp.int32, (16, 1), 0)
    position = lax.broadcasted_iota(jnp.int32, (16, BLK), 1)
    stats = jnp.zeros((8, HD), F32)

    def of_pair(pair, entry):
        a, b = 32 * pair + entry, 32 * pair + 16 + entry
        return jnp.where(sub16 < 8, query_rows[a : a + 1, :], query_rows[b : b + 1, :])

    def score(pair):
        a, b = 32 * pair, 32 * pair + 16
        queries = jnp.concatenate([query_rows[a : a + G, :], query_rows[b : b + G, :]], axis=0)
        left = jnp.concatenate(
            [jnp.where(sub16 < 8, queries, 0.0), jnp.where(sub16 < 8, 0.0, queries)], axis=1
        ).astype(BF16)
        return queries, jnp.dot(left, k_turned[pair], preferred_element_type=F32)

    def soften(pair, queries, scores):
        a, b = 2 * pair, 2 * pair + 1
        limit_a = lengths[jnp.maximum(table[0, a], 0)] - BLK * table[1, a]
        limit_b = lengths[jnp.maximum(table[0, b], 0)] - BLK * table[1, b]
        limit = jnp.where(column < 8, limit_a, limit_b)
        scores = jnp.where(position < limit, scores * SCALE, FLOOR)
        top = jnp.max(scores, axis=1, keepdims=True)
        weights = jnp.exp(scores - top)
        block_total = jnp.sum(weights, axis=1, keepdims=True)
        is_first = jnp.where(column < 8, table[1, a], table[1, b]) == 0
        own = jnp.sum(queries * of_pair(pair, G), axis=1, keepdims=True) * SCALE
        own = jnp.where(is_first, own, FLOOR)
        highest = jnp.maximum(top, own)
        factor = jnp.exp(top - highest)
        own_weight = jnp.where(is_first, jnp.exp(own - highest), 0.0)
        slot_total = block_total * factor + own_weight
        return highest, slot_total, factor, own_weight, weights.astype(BF16)

    def weigh(pair, highest, slot_total, factor, own_weight, weights):
        values = jnp.concatenate([v_v[2 * pair], v_v[2 * pair + 1]], axis=1)
        both = jnp.dot(weights, values, preferred_element_type=F32)
        block_out = jnp.where(sub16 < 8, both[:, :HD], both[:, HD:])
        slot_out = (block_out * factor + own_weight * of_pair(pair, G + 1)) / slot_total
        return slot_out.astype(BF16)

    for load in v_loads:
        load.wait()
    for c, (start, count, rows) in enumerate(CHUNKS):
        wait_bytes(recvs[c].at[others], recv_sem.at[1 + c])
        total = 0.0
        for j in range(KV):
            got = (sends[c][PEERS] if j == PEERS else recvs[c][j]).astype(jnp.int32).astype(F32)
            got = got.reshape(rows // 8, 8, HD)
            total = total + got[:-1] * (jnp.exp2(got[-1:]) * (1.0 / STEPS))
        total = total.reshape(rows - 8, HD)
        total = total.astype(BF16).astype(F32)
        per_tile = 8 // count
        for entry in range(ENTRIES):
            row = entry * count
            query_rows[pl.ds(16 * start + entry, count, stride=16), :] = total[row : row + count]

        pairs = range(start // 2, (start + count) // 2)
        ready = {}
        for pair in pairs:
            queries, scores = score(pair)
            ready[pair] = (queries, scores)
        for pair in pairs:
            ready[pair] = soften(pair, *ready[pair])
            highest, slot_total = ready[pair][:2]
            for s, part in ((2 * pair, slice(0, 8)), (2 * pair + 1, slice(8, 16))):
                stats = jnp.where(lane == s, highest[part], stats)
                stats = jnp.where(lane == 16 + s, slot_total[part], stats)
        if start + count == SLOTS:
            stats_all[PEERS] = stats
            for j, offset in enumerate(OFFSETS):
                send(7, stats_all.at[PEERS], stats_all.at[j], ahead(offset))
        for pair in pairs:
            at = 16 * pair - 8 * start
            outs[c][PEERS, at : at + 16, :] = weigh(pair, *ready[pair])
        for j, offset in enumerate(OFFSETS):
            send(4 + c, outs[c].at[PEERS], outs[c].at[j], ahead(offset))

    def side_by_side(tiles, shift):
        halves = [jnp.full((8, HD), -1.0, F32), jnp.full((8, HD), -1.0, F32)]
        for (start, count, _), first in zip(CHUNKS, LANES):
            for j in range(KV):
                half, at = divmod(first + count * j, HD)
                moved = pltpu.roll(tiles(j), (at - start - shift) % HD, 1)
                halves[half] = jnp.where((lane >= at) & (lane < at + count), moved, halves[half])
        return jnp.concatenate(halves, axis=1)

    owners = side_by_side(lambda j: first_all[j], OWNER_LANE)
    belongs = lax.broadcasted_iota(jnp.int32, (ROWS, 2 * HD), 0).astype(F32) == owners[0:1]

    wait_bytes(stats_all.at[others], recv_sem.at[7])
    tops = side_by_side(lambda j: stats_all[j], 0)
    totals = side_by_side(lambda j: stats_all[j], 16)
    shares = []
    for g in range(G):
        masked = jnp.where(belongs, tops[g : g + 1], -3e38)
        highest = jnp.max(masked, axis=1, keepdims=True)
        share = jnp.exp(masked - highest) * totals[g : g + 1]
        upper = share.astype(BF16)
        lower = (share - upper.astype(F32)).astype(BF16)
        shares.append(jnp.concatenate([upper, lower], axis=0))

    def arrived(c):
        wait_bytes(outs[c].at[others], recv_sem.at[4 + c])
        wides[c][...] = outs[c][...].astype(F32).reshape(wides[c].shape)

    def slots_of(c, g):
        return wides[c][pl.ds(g, wides[c].shape[0] // G, stride=G), :].astype(BF16)

    for c in range(len(CHUNKS)):
        arrived(c)
    ones = jnp.ones((2 * HD, HD), BF16)
    attended = []
    for g in range(G):
        slots = [slots_of(c, g) for c in sorted(range(len(CHUNKS)), key=lambda c: LANES[c])]
        slots = jnp.concatenate(slots + [jnp.zeros((2 * HD - KV * SLOTS, HD), BF16)], axis=0)
        both = jnp.dot(
            shares[g], jnp.concatenate([slots, ones], axis=1), preferred_element_type=F32
        )
        both = both[:ROWS] + both[ROWS:]
        attended.append((both[:, :HD] / both[:, HD:]).astype(BF16))
    attended = jnp.concatenate(attended, axis=1)

    loads[3].wait()
    mine = pl.ds(pl.multiple_of(core * HALF, HALF), HALF)
    theirs = pl.ds(pl.multiple_of((1 - core) * HALF, HALF), HALF)
    half_send[...] = jnp.dot(attended, w_out[:, theirs], preferred_element_type=F32)
    send(8, half_send, half_recv, sibling)
    own_half = jnp.dot(attended, w_out[:, mine], preferred_element_type=F32)
    wait_bytes(half_recv, recv_sem.at[8])
    z_all[my_z] = (own_half + half_recv[...]).astype(BF16)
    for peer in z_peers:
        send(9, z_all.at[my_z], z_all.at[my_z], peer)
    wait_bytes(z_all.at[pl.ds(0, SIDE - 1)], recv_sem.at[9])
    parts = [z_all[z].astype(F32) for z in range(SIDE)]
    done = (((parts[0] + parts[1]) + parts[2]) + parts[3]).astype(BF16)
    done_send[...] = done
    send(10, done_send, out_ref.at[:, mine], sibling)
    keep = pltpu.make_async_copy(done_send, out_ref.at[:, mine], load_sem.at[6])
    keep.start()

    wait_bytes(first_all.at[others], send_sem.at[0])
    for c, (start, count, rows) in enumerate(CHUNKS):
        wait_bytes(sends[c].at[others], send_sem.at[1 + c])
        wait_bytes(outs[c].at[others], send_sem.at[4 + c])
    wait_bytes(stats_all.at[others], send_sem.at[7])
    wait_bytes(half_send, send_sem.at[8])
    wait_bytes(z_all.at[pl.ds(0, SIDE - 1)], send_sem.at[9])
    wait_bytes(done_send, send_sem.at[10])
    wait_bytes(out_ref.at[:, theirs], recv_sem.at[10])
    keep.wait()


def per_device(tokens, gain, w_qkv, w_out, k_cache, v_cache, lengths, block_table):
    features = tokens.shape[1]
    anywhere = pl.BlockSpec(memory_space=pl.ANY)
    return pl.pallas_call(
        kernel,
        out_shape=pltpu.VMEM((ROWS, features), BF16),
        in_specs=[anywhere] * 8,
        out_specs=pl.BlockSpec(memory_space=pltpu.VMEM),
        scratch_shapes=[
            pltpu.VMEM((ROWS, features), BF16),
            pltpu.VMEM((1, features), F32),
            pltpu.VMEM((features, ENTRIES * HD), BF16),
            pltpu.VMEM((G * HD, features), BF16),
            pltpu.VMEM((SLOTS, BLK, HD), BF16),
            pltpu.VMEM((SLOTS // 2, 2 * HD, BLK), BF16),
            pltpu.VMEM((SLOTS, BLK, HD), BF16),
            pltpu.VMEM((KV, 8, HD), F32),
        ]
        + [pltpu.VMEM((KV, rows, HD), jnp.int16) for _, _, rows in CHUNKS]
        + [pltpu.VMEM((PEERS, rows, HD), jnp.int16) for _, _, rows in CHUNKS]
        + [
            pltpu.VMEM((SLOTS * 16, HD), F32),
        ]
        + [pltpu.VMEM((KV, count * G, HD), BF16) for _, count, _ in CHUNKS]
        + [pltpu.VMEM((KV, 8, HD), F32)]
        + [pltpu.VMEM((KV * count * G, HD), F32) for _, count, _ in CHUNKS]
        + [
            pltpu.VMEM((ROWS, HALF), F32),
            pltpu.VMEM((ROWS, HALF), F32),
            pltpu.VMEM((SIDE, ROWS, HALF), BF16),
            pltpu.VMEM((ROWS, HALF), BF16),
            pltpu.SMEM((ROWS,), jnp.int32),
            pltpu.SMEM((2, SLOTS), jnp.int32),
            pltpu.SemaphoreType.DMA((7,)),
            pltpu.SemaphoreType.DMA((2, SLOTS // 2)),
            pltpu.SemaphoreType.DMA((11,)),
            pltpu.SemaphoreType.DMA((11,)),
        ],
        compiler_params=pltpu.CompilerParams(
            collective_id=0, has_side_effects=True, vmem_limit_bytes=56 << 20
        ),
    )(
        tokens,
        gain.reshape(1, features),
        w_qkv.reshape(features, ENTRIES * HD),
        w_out.reshape(G * HD, features),
        k_cache.reshape(SLOTS, BLK, HD),
        v_cache.reshape(SLOTS, BLK, HD),
        lengths,
        block_table.T,
    )


def solution(mesh):
    placed = (
        P(None, "kv"),
        P("kv"),
        P("kv", "tp", None),
        P("tp", None, "kv"),
        P("tp", "kv", None, None),
        P("tp", "kv", None, None),
        P(),
        P("kv", None),
    )
    return jax.shard_map(
        per_device, mesh=mesh, in_specs=placed, out_specs=P(None, "kv"), check_vma=False
    )
```

```python
import functools

import jax
import jax.numpy as jnp
from jax import lax
from jax.experimental import pallas as pl
from jax.experimental.pallas import tpu as pltpu
from jax.sharding import PartitionSpec as P

D = 8192
HD = 128
G = 8
ROWS = 64
SLOTS = 10
ENTRIES = G + 2
BLK = 4096
SIDE = 4
KV = SIDE * SIDE
PEERS = KV - 1
HALF = 256

EPSILON = 1e-05
FLOOR = -1e30
SCALE = HD ** (-0.5)

MESH = pl.DeviceIdType.MESH
F32 = jnp.float32
BF16 = jnp.bfloat16

SQUARE_LANE = 8
OWNER_LANE = 16

EARLY_VALUES = 1
EARLY_KEYS = 3
TURN = 512

CHUNKS = ((0, 4, 48), (4, 4, 48), (8, 2, 16))
LANES = (0, 64, 128)
TOP_LANES = (0, 64, 32)
TOTAL_LANES = (16, 80, 96)

STEPS = 32000.0


def ring_distance(step):
    return min(step, SIDE - step)


OFFSETS = sorted(
    [(a, b) for a in range(SIDE) for b in range(SIDE) if (a, b) != (0, 0)],
    key=lambda m: -(ring_distance(m[0]) + ring_distance(m[1])),
)


def wait_bytes(ref, sem):
    pltpu.make_async_copy(ref, ref, sem).wait()


def kernel(
    tokens_hbm,
    gain_hbm,
    w_qkv_hbm,
    w_out_hbm,
    k_hbm,
    v_hbm,
    lengths_hbm,
    table_hbm,
    out_ref,
    tokens_v,
    gain_v,
    w_qkv,
    w_out,
    k_v,
    k_turned,
    v_v,
    first_all,
    send0,
    send1,
    send2,
    recv0,
    recv1,
    recv2,
    query_rows,
    outs0,
    outs1,
    outs2,
    stats_all,
    wide0,
    wide1,
    wide2,
    half_send,
    half_recv,
    z_all,
    done_send,
    lengths,
    table,
    load_sem,
    kv_sem,
    send_sem,
    recv_sem,
):
    me = lax.axis_index("kv")
    my_x, my_y = me // SIDE, me % SIDE
    tp = lax.axis_index("tp")
    my_z, core = tp // 2, tp % 2

    def ahead(offset):
        return {"kv": ((my_x + offset[0]) % SIDE) * SIDE + (my_y + offset[1]) % SIDE}

    def behind(offset):
        return ahead(((SIDE - offset[0]) % SIDE, (SIDE - offset[1]) % SIDE))

    sibling = {"tp": my_z * 2 + (1 - core)}
    z_peers = [{"tp": ((my_z + step) % SIDE) * 2 + core} for step in (2, 1, 3)]

    barrier = pltpu.get_barrier_semaphore()
    for offset in OFFSETS:
        pl.semaphore_signal(barrier, inc=1, device_id=ahead(offset), device_id_type=MESH)
    for peer in z_peers + [sibling]:
        pl.semaphore_signal(barrier, inc=1, device_id=peer, device_id_type=MESH)

    loads = [
        pltpu.make_async_copy(tokens_hbm, tokens_v, load_sem.at[0]),
        pltpu.make_async_copy(gain_hbm, gain_v, load_sem.at[1]),
        pltpu.make_async_copy(w_qkv_hbm, w_qkv, load_sem.at[2]),
        pltpu.make_async_copy(w_out_hbm, w_out, load_sem.at[3]),
        pltpu.make_async_copy(table_hbm, table, load_sem.at[4]),
        pltpu.make_async_copy(lengths_hbm, lengths, load_sem.at[5]),
    ]
    k_loads, v_loads = [], []
    for pair in range(SLOTS // 2):
        part = pl.ds(2 * pair, 2)
        k_loads.append(pltpu.make_async_copy(k_hbm.at[part], k_v.at[part], kv_sem.at[0, pair]))
        v_loads.append(pltpu.make_async_copy(v_hbm.at[part], v_v.at[part], kv_sem.at[1, pair]))
    for load in loads[:3] + loads[4:]:
        load.start()
    for pair in range(SLOTS // 2):
        k_loads[pair].start()
    for pair in range(EARLY_VALUES):
        v_loads[pair].start()

    sub = lax.broadcasted_iota(jnp.int32, (8, HD), 0)
    lane = lax.broadcasted_iota(jnp.int32, (8, HD), 1)

    loads[0].wait()
    tokens = tokens_v[...].astype(F32)
    squares = jnp.sum(tokens * tokens, axis=1, keepdims=True)
    loads[4].wait()
    loads[5].wait()
    owners = jnp.full((8, HD), -1, jnp.int32)
    for slot in range(SLOTS):
        owners = jnp.where(lane == OWNER_LANE + slot, table[0, slot], owners)
    for c, (start, count, _) in enumerate(CHUNKS):
        for s in range(count):
            owners = jnp.where((lane == c) & (sub % count == s), table[0, start + s], owners)
    tile = owners.astype(F32)
    for k in range(ROWS // 8):
        tile = jnp.where(lane == SQUARE_LANE + k, squares[8 * k : 8 * k + 8], tile)
    first_all[PEERS] = tile

    pl.semaphore_wait(barrier, PEERS + 4)

    def send(phase, src, dst, peer):
        pltpu.make_async_remote_copy(
            src_ref=src,
            dst_ref=dst,
            send_sem=send_sem.at[phase],
            recv_sem=recv_sem.at[phase],
            device_id=peer,
            device_id_type=MESH,
        ).start()

    others = pl.ds(0, PEERS)

    for j, offset in enumerate(OFFSETS):
        send(0, first_all.at[PEERS], first_all.at[j], ahead(offset))

    def turn_keys(pair):
        k_loads[pair].wait()
        for half in range(2):
            for at in range(0, BLK, TURN):
                k_turned[pair, HD * half : HD * half + HD, at : at + TURN] = k_v[
                    2 * pair + half, at : at + TURN
                ].T

    for pair in range(EARLY_KEYS):
        turn_keys(pair)
    loads[1].wait()
    loads[2].wait()
    wait_bytes(first_all.at[others], recv_sem.at[0])

    for pair in range(EARLY_VALUES, SLOTS // 2):
        v_loads[pair].start()
    loads[3].start()
    squares = first_all[0]
    for j in range(1, KV):
        squares = squares + first_all[j]
    inverse = lax.rsqrt(squares / D + EPSILON)
    gains = gain_v[...]
    normed = jnp.concatenate(
        [tokens[8 * k : 8 * k + 8] * inverse[:, SQUARE_LANE + k : SQUARE_LANE + k + 1] * gains for k in range(ROWS // 8)], axis=0
    ).astype(BF16)
    partial = jnp.dot(normed, w_qkv[...], preferred_element_type=F32)
    largest = jnp.max(jnp.abs(partial), axis=1, keepdims=True)
    exponent = jnp.ceil(jnp.log2(jnp.maximum(largest, 1e-30)))
    whole = jnp.round(partial * (STEPS * jnp.exp2(-exponent)))
    coarse = jnp.floor(whole * (1.0 / 256.0))
    fine = whole - 256.0 * coarse
    stacked = jnp.concatenate([coarse, fine], axis=0).astype(BF16)
    exponents = jnp.broadcast_to(exponent, (ROWS, HD))
    exponents = jnp.concatenate([jnp.zeros_like(exponents), exponents], axis=0).astype(BF16)

    row_of_lane = lax.broadcasted_iota(jnp.int32, (KV * 8, HD), 1)
    row_number = (row_of_lane % ROWS).astype(F32)
    part_weight = jnp.where(row_of_lane < ROWS, 256.0, 1.0)
    everyone = first_all[...].reshape(KV * 8, HD)
    sub3 = lax.broadcasted_iota(jnp.int32, (KV, 8, HD), 1)
    sends = (send0, send1, send2)
    recvs = (recv0, recv1, recv2)
    outs = (outs0, outs1, outs2)
    wides = (wide0, wide1, wide2)
    picks = [
        jnp.where(everyone[:, c : c + 1] == row_number, part_weight, 0.0).astype(BF16)
        for c in range(len(CHUNKS))
    ]

    def packed(c):
        _, count, _ = CHUNKS[c]
        got = jnp.dot(picks[c], stacked, preferred_element_type=F32).reshape(KV, 8, ENTRIES * HD)
        per_tile = 8 // count
        tiles = []
        for first in range(0, ENTRIES, per_tile):
            tile = got[:, :, first * HD : (first + 1) * HD]
            for e in range(1, min(per_tile, ENTRIES - first)):
                tile = jnp.where(
                    sub3 >= e * count, got[:, :, (first + e) * HD : (first + e + 1) * HD], tile
                )
            tiles.append(tile)
        return tiles

    def send_rows(c, tiles):
        sends[c][...] = jnp.concatenate(tiles, axis=1).astype(jnp.int32).astype(jnp.int16)
        for j, offset in enumerate(OFFSETS):
            send(1 + c, sends[c].at[j], recvs[c].at[j], behind(offset))

    lane3 = lax.broadcasted_iota(jnp.int32, (KV, 8, HD), 2)
    marks = jnp.zeros((KV, 8, HD), F32)
    for c, pick in enumerate(picks):
        mark = jnp.dot(pick, exponents, preferred_element_type=F32).reshape(KV, 8, HD)
        marks = jnp.where(lane3 == c, mark, marks)
    send_rows(0, packed(0) + [marks])
    last_tiles = packed(2)
    send_rows(1, packed(1) + last_tiles[:1])
    send_rows(2, last_tiles[1:])

    for pair in range(EARLY_KEYS, SLOTS // 2):
        turn_keys(pair)

    sub16 = lax.broadcasted_iota(jnp.int32, (16, HD), 0)
    column = lax.broadcasted_iota(jnp.int32, (16, 1), 0)
    position = lax.broadcasted_iota(jnp.int32, (16, BLK), 1)
    stats = jnp.zeros((8, HD), F32)

    def of_pair(pair, entry):
        a, b = 32 * pair + entry, 32 * pair + 16 + entry
        return jnp.where(sub16 < 8, query_rows[a : a + 1, :], query_rows[b : b + 1, :])

    def score(pair):
        a, b = 32 * pair, 32 * pair + 16
        queries = jnp.concatenate([query_rows[a : a + G, :], query_rows[b : b + G, :]], axis=0)
        left = jnp.concatenate(
            [jnp.where(sub16 < 8, queries, 0.0), jnp.where(sub16 < 8, 0.0, queries)], axis=1
        ).astype(BF16)
        return queries, jnp.dot(left, k_turned[pair], preferred_element_type=F32)

    def soften(pair, queries, scores):
        a, b = 2 * pair, 2 * pair + 1
        limit_a = lengths[jnp.maximum(table[0, a], 0)] - BLK * table[1, a]
        limit_b = lengths[jnp.maximum(table[0, b], 0)] - BLK * table[1, b]
        limit = jnp.where(column < 8, limit_a, limit_b)
        scores = jnp.where(position < limit, scores * SCALE, FLOOR)
        top = jnp.max(scores, axis=1, keepdims=True)
        weights = jnp.exp(scores - top)
        block_total = jnp.sum(weights, axis=1, keepdims=True)
        is_first = jnp.where(column < 8, table[1, a], table[1, b]) == 0
        own = jnp.sum(queries * of_pair(pair, G), axis=1, keepdims=True) * SCALE
        own = jnp.where(is_first, own, FLOOR)
        highest = jnp.maximum(top, own)
        factor = jnp.exp(top - highest)
        own_weight = jnp.where(is_first, jnp.exp(own - highest), 0.0)
        slot_total = block_total * factor + own_weight
        return highest, slot_total, factor, own_weight, weights.astype(BF16)

    def weigh(pair, highest, slot_total, factor, own_weight, weights):
        values = jnp.concatenate([v_v[2 * pair], v_v[2 * pair + 1]], axis=1)
        both = jnp.dot(weights, values, preferred_element_type=F32)
        block_out = jnp.where(sub16 < 8, both[:, :HD], both[:, HD:])
        slot_out = (block_out * factor + own_weight * of_pair(pair, G + 1)) / slot_total
        return slot_out.astype(BF16)

    for load in v_loads:
        load.wait()
    for c, (start, count, rows) in enumerate(CHUNKS):
        wait_bytes(recvs[c].at[others], recv_sem.at[1 + c])
        total = 0.0
        for j in range(KV):
            first, second, third = (
                sends[i].at[PEERS] if j == PEERS else recvs[i].at[j] for i in range(len(CHUNKS))
            )
            scale = jnp.exp2(first[32:48].astype(jnp.int32).astype(F32)[8:, c : c + 1]) * (1.0 / STEPS)
            if c < 2:
                got = (first, second)[c][...].astype(jnp.int32).astype(F32)[:40]
            else:
                got = jnp.concatenate(
                    [
                        second[32:48].astype(jnp.int32).astype(F32)[8:],
                        third[...].astype(jnp.int32).astype(F32),
                    ],
                    axis=0,
                )
            total = total + got.reshape(got.shape[0] // 8, 8, HD) * scale
        total = total.reshape(total.shape[0] * 8, HD)
        total = total.astype(BF16).astype(F32)
        per_tile = 8 // count
        for entry in range(ENTRIES):
            row = entry * count
            query_rows[pl.ds(16 * start + entry, count, stride=16), :] = total[row : row + count]

        pairs = range(start // 2, (start + count) // 2)
        ready = {}
        for pair in pairs:
            queries, scores = score(pair)
            ready[pair] = (queries, scores)
        for pair in pairs:
            ready[pair] = soften(pair, *ready[pair])
            highest, slot_total = ready[pair][:2]
            for s, part in ((2 * pair, slice(0, 8)), (2 * pair + 1, slice(8, 16))):
                stats = jnp.where(lane == TOP_LANES[c] + s - start, highest[part], stats)
                stats = jnp.where(lane == TOTAL_LANES[c] + s - start, slot_total[part], stats)
        if start + count == SLOTS:
            stats_all[PEERS] = stats
            for j, offset in enumerate(OFFSETS):
                send(7, stats_all.at[PEERS], stats_all.at[j], ahead(offset))
        for pair in pairs:
            at = 16 * pair - 8 * start
            outs[c][PEERS, at : at + 16, :] = weigh(pair, *ready[pair])
        for j, offset in enumerate(OFFSETS):
            send(4 + c, outs[c].at[PEERS], outs[c].at[j], ahead(offset))

    def side_by_side(tiles, shift):
        halves = [jnp.full((8, HD), -1.0, F32), jnp.full((8, HD), -1.0, F32)]
        for (start, count, _), first in zip(CHUNKS, LANES):
            for j in range(KV):
                half, at = divmod(first + count * j, HD)
                moved = pltpu.roll(tiles(j), (at - start - shift) % HD, 1)
                halves[half] = jnp.where((lane >= at) & (lane < at + count), moved, halves[half])
        return jnp.concatenate(halves, axis=1)

    owners = side_by_side(lambda j: first_all[j], OWNER_LANE)
    belongs = lax.broadcasted_iota(jnp.int32, (ROWS, 2 * HD), 0).astype(F32) == owners[0:1]

    wait_bytes(stats_all.at[others], recv_sem.at[7])
    def placed(shift, count):
        tile = jnp.full((8, HD), -1.0, F32)
        group = (lane % 64) // count
        for j in range(KV):
            tile = jnp.where(group == j, pltpu.roll(stats_all[j], (count * j - shift) % HD, 1), tile)
        return tile

    last = placed(TOP_LANES[2], 2)
    tops = jnp.concatenate([placed(TOP_LANES[0], 4), last], axis=1)
    totals = jnp.concatenate([placed(TOTAL_LANES[0], 4), pltpu.roll(last, 64, 1)], axis=1)
    shares = []
    for g in range(G):
        masked = jnp.where(belongs, tops[g : g + 1], -3e38)
        highest = jnp.max(masked, axis=1, keepdims=True)
        share = jnp.exp(masked - highest) * totals[g : g + 1]
        upper = share.astype(BF16)
        lower = (share - upper.astype(F32)).astype(BF16)
        shares.append(jnp.concatenate([upper, lower], axis=0))

    def arrived(c):
        wait_bytes(outs[c].at[others], recv_sem.at[4 + c])
        wides[c][...] = outs[c][...].astype(F32).reshape(wides[c].shape)

    def slots_of(c, g):
        return wides[c][pl.ds(g, wides[c].shape[0] // G, stride=G), :].astype(BF16)

    for c in range(len(CHUNKS)):
        arrived(c)
    ones = jnp.ones((2 * HD, HD), BF16)
    attended = []
    for g in range(G):
        slots = [slots_of(c, g) for c in sorted(range(len(CHUNKS)), key=lambda c: LANES[c])]
        slots = jnp.concatenate(slots + [jnp.zeros((2 * HD - KV * SLOTS, HD), BF16)], axis=0)
        both = jnp.dot(
            shares[g], jnp.concatenate([slots, ones], axis=1), preferred_element_type=F32
        )
        both = both[:ROWS] + both[ROWS:]
        attended.append((both[:, :HD] / both[:, HD:]).astype(BF16))
    attended = jnp.concatenate(attended, axis=1)

    loads[3].wait()
    mine = pl.ds(pl.multiple_of(core * HALF, HALF), HALF)
    theirs = pl.ds(pl.multiple_of((1 - core) * HALF, HALF), HALF)
    half_send[...] = jnp.dot(attended, w_out[:, theirs], preferred_element_type=F32)
    send(8, half_send, half_recv, sibling)
    own_half = jnp.dot(attended, w_out[:, mine], preferred_element_type=F32)
    wait_bytes(half_recv, recv_sem.at[8])
    z_all[my_z] = (own_half + half_recv[...]).astype(BF16)
    for peer in z_peers:
        send(9, z_all.at[my_z], z_all.at[my_z], peer)
    wait_bytes(first_all.at[others], send_sem.at[0])
    for c, (start, count, rows) in enumerate(CHUNKS):
        wait_bytes(sends[c].at[others], send_sem.at[1 + c])
        wait_bytes(outs[c].at[others], send_sem.at[4 + c])
    wait_bytes(stats_all.at[others], send_sem.at[7])
    wait_bytes(half_send, send_sem.at[8])
    wait_bytes(z_all.at[pl.ds(0, SIDE - 1)], recv_sem.at[9])
    parts = [z_all[z].astype(F32) for z in range(SIDE)]
    done = (((parts[0] + parts[1]) + parts[2]) + parts[3]).astype(BF16)
    done_send[...] = done
    send(10, done_send, out_ref.at[:, mine], sibling)
    out_ref[:, mine] = done
    wait_bytes(z_all.at[pl.ds(0, SIDE - 1)], send_sem.at[9])
    wait_bytes(done_send, send_sem.at[10])
    wait_bytes(out_ref.at[:, theirs], recv_sem.at[10])


def per_device(tokens, gain, w_qkv, w_out, k_cache, v_cache, lengths, block_table):
    features = tokens.shape[1]
    anywhere = pl.BlockSpec(memory_space=pl.ANY)
    return pl.pallas_call(
        kernel,
        out_shape=pltpu.VMEM((ROWS, features), BF16),
        in_specs=[anywhere] * 8,
        out_specs=pl.BlockSpec(memory_space=pltpu.VMEM),
        scratch_shapes=[
            pltpu.VMEM((ROWS, features), BF16),
            pltpu.VMEM((1, features), F32),
            pltpu.VMEM((features, ENTRIES * HD), BF16),
            pltpu.VMEM((G * HD, features), BF16),
            pltpu.VMEM((SLOTS, BLK, HD), BF16),
            pltpu.VMEM((SLOTS // 2, 2 * HD, BLK), BF16),
            pltpu.VMEM((SLOTS, BLK, HD), BF16),
            pltpu.VMEM((KV, 8, HD), F32),
        ]
        + [pltpu.VMEM((KV, rows, HD), jnp.int16) for _, _, rows in CHUNKS]
        + [pltpu.VMEM((PEERS, rows, HD), jnp.int16) for _, _, rows in CHUNKS]
        + [
            pltpu.VMEM((SLOTS * 16, HD), F32),
        ]
        + [pltpu.VMEM((KV, count * G, HD), BF16) for _, count, _ in CHUNKS]
        + [pltpu.VMEM((KV, 8, HD), F32)]
        + [pltpu.VMEM((KV * count * G, HD), F32) for _, count, _ in CHUNKS]
        + [
            pltpu.VMEM((ROWS, HALF), F32),
            pltpu.VMEM((ROWS, HALF), F32),
            pltpu.VMEM((SIDE, ROWS, HALF), BF16),
            pltpu.VMEM((ROWS, HALF), BF16),
            pltpu.SMEM((ROWS,), jnp.int32),
            pltpu.SMEM((2, SLOTS), jnp.int32),
            pltpu.SemaphoreType.DMA((6,)),
            pltpu.SemaphoreType.DMA((2, SLOTS // 2)),
            pltpu.SemaphoreType.DMA((11,)),
            pltpu.SemaphoreType.DMA((11,)),
        ],
        compiler_params=pltpu.CompilerParams(
            collective_id=0, has_side_effects=True, vmem_limit_bytes=56 << 20
        ),
    )(
        tokens,
        gain.reshape(1, features),
        w_qkv.reshape(features, ENTRIES * HD),
        w_out.reshape(G * HD, features),
        k_cache.reshape(SLOTS, BLK, HD),
        v_cache.reshape(SLOTS, BLK, HD),
        lengths,
        block_table.T,
    )


def solution(mesh):
    placed = (
        P(None, "kv"),
        P("kv"),
        P("kv", "tp", None),
        P("tp", None, "kv"),
        P("tp", "kv", None, None),
        P("tp", "kv", None, None),
        P(),
        P("kv", None),
    )
    return jax.shard_map(
        per_device, mesh=mesh, in_specs=placed, out_specs=P(None, "kv"), check_vma=False
    )
```

```python
import functools

import jax
import jax.numpy as jnp
from jax import lax
from jax.experimental import pallas as pl
from jax.experimental.pallas import tpu as pltpu
from jax.sharding import PartitionSpec as P

D = 8192
HD = 128
G = 8
ROWS = 64
SLOTS = 10
ENTRIES = G + 2
BLK = 4096
SIDE = 4
KV = SIDE * SIDE
PEERS = KV - 1
HALF = 256

EPSILON = 1e-05
FLOOR = -1e30
SCALE = HD ** (-0.5)

MESH = pl.DeviceIdType.MESH
F32 = jnp.float32
BF16 = jnp.bfloat16

SQUARE_LANE = 8
OWNER_LANE = 16

EARLY_VALUES = 1
EARLY_KEYS = 3
TURN = 512

CHUNKS = ((0, 4, 48), (4, 4, 48), (8, 2, 16))
LANES = (0, 64, 128)
TOP_LANES = (0, 64, 32)
TOTAL_LANES = (16, 80, 96)

STEPS = 32000.0


def ring_distance(step):
    return min(step, SIDE - step)


OFFSETS = sorted(
    [(a, b) for a in range(SIDE) for b in range(SIDE) if (a, b) != (0, 0)],
    key=lambda m: -(ring_distance(m[0]) + ring_distance(m[1])),
)


def wait_bytes(ref, sem):
    pltpu.make_async_copy(ref, ref, sem).wait()


def kernel(
    tokens_hbm,
    gain_hbm,
    w_qkv_hbm,
    w_out_hbm,
    k_hbm,
    v_hbm,
    lengths_hbm,
    table_hbm,
    out_ref,
    tokens_v,
    gain_v,
    w_qkv,
    w_out,
    k_v,
    k_turned,
    v_v,
    first_all,
    send0,
    send1,
    send2,
    recv0,
    recv1,
    recv2,
    query_rows,
    outs0,
    outs1,
    outs2,
    stats_all,
    wide0,
    wide1,
    wide2,
    half_send,
    half_recv,
    z_all,
    done_send,
    lengths,
    table,
    load_sem,
    kv_sem,
    send_sem,
    recv_sem,
):
    me = lax.axis_index("kv")
    my_x, my_y = me // SIDE, me % SIDE
    tp = lax.axis_index("tp")
    my_z, core = tp // 2, tp % 2

    def ahead(offset):
        return {"kv": ((my_x + offset[0]) % SIDE) * SIDE + (my_y + offset[1]) % SIDE}

    def behind(offset):
        return ahead(((SIDE - offset[0]) % SIDE, (SIDE - offset[1]) % SIDE))

    sibling = {"tp": my_z * 2 + (1 - core)}
    z_peers = [{"tp": ((my_z + step) % SIDE) * 2 + core} for step in (2, 1, 3)]

    barrier = pltpu.get_barrier_semaphore()
    for offset in OFFSETS:
        pl.semaphore_signal(barrier, inc=1, device_id=ahead(offset), device_id_type=MESH)
    for peer in z_peers + [sibling]:
        pl.semaphore_signal(barrier, inc=1, device_id=peer, device_id_type=MESH)

    loads = [
        pltpu.make_async_copy(tokens_hbm, tokens_v, load_sem.at[0]),
        pltpu.make_async_copy(gain_hbm, gain_v, load_sem.at[1]),
        pltpu.make_async_copy(w_qkv_hbm, w_qkv, load_sem.at[2]),
        pltpu.make_async_copy(w_out_hbm, w_out, load_sem.at[3]),
        pltpu.make_async_copy(table_hbm, table, load_sem.at[4]),
        pltpu.make_async_copy(lengths_hbm, lengths, load_sem.at[5]),
    ]
    k_loads, v_loads = [], []
    for pair in range(SLOTS // 2):
        part = pl.ds(2 * pair, 2)
        k_loads.append(pltpu.make_async_copy(k_hbm.at[part], k_v.at[part], kv_sem.at[0, pair]))
        v_loads.append(pltpu.make_async_copy(v_hbm.at[part], v_v.at[part], kv_sem.at[1, pair]))
    for load in loads[:3] + loads[4:]:
        load.start()
    for pair in range(SLOTS // 2):
        k_loads[pair].start()
    for pair in range(EARLY_VALUES):
        v_loads[pair].start()

    sub = lax.broadcasted_iota(jnp.int32, (8, HD), 0)
    lane = lax.broadcasted_iota(jnp.int32, (8, HD), 1)

    loads[0].wait()
    tokens = tokens_v[...].astype(F32)
    squares = jnp.sum(tokens * tokens, axis=1, keepdims=True)
    loads[4].wait()
    loads[5].wait()
    owners = jnp.full((8, HD), -1, jnp.int32)
    for slot in range(SLOTS):
        owners = jnp.where(lane == OWNER_LANE + slot, table[0, slot], owners)
    for c, (start, count, _) in enumerate(CHUNKS):
        for s in range(count):
            owners = jnp.where((lane == c) & (sub % count == s), table[0, start + s], owners)
    tile = owners.astype(F32)
    for k in range(ROWS // 8):
        tile = jnp.where(lane == SQUARE_LANE + k, squares[8 * k : 8 * k + 8], tile)
    first_all[PEERS] = tile

    pl.semaphore_wait(barrier, PEERS + 4)

    def send(phase, src, dst, peer):
        pltpu.make_async_remote_copy(
            src_ref=src,
            dst_ref=dst,
            send_sem=send_sem.at[phase],
            recv_sem=recv_sem.at[phase],
            device_id=peer,
            device_id_type=MESH,
        ).start()

    others = pl.ds(0, PEERS)

    for j, offset in enumerate(OFFSETS):
        send(0, first_all.at[PEERS], first_all.at[j], ahead(offset))

    def turn_keys(pair):
        k_loads[pair].wait()
        for half in range(2):
            for at in range(0, BLK, TURN):
                k_turned[pair, HD * half : HD * half + HD, at : at + TURN] = k_v[
                    2 * pair + half, at : at + TURN
                ].T

    for pair in range(EARLY_KEYS):
        turn_keys(pair)
    loads[1].wait()
    loads[2].wait()
    wait_bytes(first_all.at[others], recv_sem.at[0])

    for pair in range(EARLY_VALUES, SLOTS // 2):
        v_loads[pair].start()
    loads[3].start()
    squares = first_all[0]
    for j in range(1, KV):
        squares = squares + first_all[j]
    inverse = lax.rsqrt(squares / D + EPSILON)
    gains = gain_v[...]
    normed = jnp.concatenate(
        [tokens[8 * k : 8 * k + 8] * inverse[:, SQUARE_LANE + k : SQUARE_LANE + k + 1] * gains for k in range(ROWS // 8)], axis=0
    ).astype(BF16)
    partial = jnp.dot(normed, w_qkv[...], preferred_element_type=F32)
    largest = jnp.max(jnp.abs(partial), axis=1, keepdims=True)
    exponent = jnp.ceil(jnp.log2(jnp.maximum(largest, 1e-30)))
    whole = jnp.round(partial * (STEPS * jnp.exp2(-exponent)))
    coarse = jnp.floor(whole * (1.0 / 256.0))
    fine = whole - 256.0 * coarse
    stacked = jnp.concatenate([coarse, fine], axis=0).astype(BF16)
    exponents = jnp.broadcast_to(exponent, (ROWS, HD))
    exponents = jnp.concatenate([jnp.zeros_like(exponents), exponents], axis=0).astype(BF16)

    row_of_lane = lax.broadcasted_iota(jnp.int32, (KV * 8, HD), 1)
    row_number = (row_of_lane % ROWS).astype(F32)
    part_weight = jnp.where(row_of_lane < ROWS, 256.0, 1.0)
    everyone = first_all[...].reshape(KV * 8, HD)
    sub3 = lax.broadcasted_iota(jnp.int32, (KV, 8, HD), 1)
    sends = (send0, send1, send2)
    recvs = (recv0, recv1, recv2)
    outs = (outs0, outs1, outs2)
    wides = (wide0, wide1, wide2)
    picks = [
        jnp.where(everyone[:, c : c + 1] == row_number, part_weight, 0.0).astype(BF16)
        for c in range(len(CHUNKS))
    ]

    def packed(c):
        _, count, _ = CHUNKS[c]
        got = jnp.dot(picks[c], stacked, preferred_element_type=F32).reshape(KV, 8, ENTRIES * HD)
        per_tile = 8 // count
        tiles = []
        for first in range(0, ENTRIES, per_tile):
            tile = got[:, :, first * HD : (first + 1) * HD]
            for e in range(1, min(per_tile, ENTRIES - first)):
                tile = jnp.where(
                    sub3 >= e * count, got[:, :, (first + e) * HD : (first + e + 1) * HD], tile
                )
            tiles.append(tile)
        return tiles

    def send_rows(c, tiles):
        sends[c][...] = jnp.concatenate(tiles, axis=1).astype(jnp.int32).astype(jnp.int16)
        for j, offset in enumerate(OFFSETS):
            send(1 + c, sends[c].at[j], recvs[c].at[j], behind(offset))

    lane3 = lax.broadcasted_iota(jnp.int32, (KV, 8, HD), 2)
    marks = jnp.zeros((KV, 8, HD), F32)
    for c, pick in enumerate(picks):
        mark = jnp.dot(pick, exponents, preferred_element_type=F32).reshape(KV, 8, HD)
        marks = jnp.where(lane3 == c, mark, marks)
    send_rows(0, packed(0) + [marks])
    last_tiles = packed(2)
    send_rows(1, packed(1) + last_tiles[:1])
    send_rows(2, last_tiles[1:])

    for pair in range(EARLY_KEYS, SLOTS // 2):
        turn_keys(pair)

    sub16 = lax.broadcasted_iota(jnp.int32, (16, HD), 0)
    column = lax.broadcasted_iota(jnp.int32, (16, 1), 0)
    position = lax.broadcasted_iota(jnp.int32, (16, BLK), 1)
    stats = jnp.zeros((8, HD), F32)

    def of_pair(pair, entry):
        a, b = 32 * pair + entry, 32 * pair + 16 + entry
        return jnp.where(sub16 < 8, query_rows[a : a + 1, :], query_rows[b : b + 1, :])

    def score(pair):
        a, b = 32 * pair, 32 * pair + 16
        queries = jnp.concatenate([query_rows[a : a + G, :], query_rows[b : b + G, :]], axis=0)
        left = jnp.concatenate(
            [jnp.where(sub16 < 8, queries, 0.0), jnp.where(sub16 < 8, 0.0, queries)], axis=1
        ).astype(BF16)
        return queries, jnp.dot(left, k_turned[pair], preferred_element_type=F32)

    def soften(pair, queries, scores):
        a, b = 2 * pair, 2 * pair + 1
        limit_a = lengths[jnp.maximum(table[0, a], 0)] - BLK * table[1, a]
        limit_b = lengths[jnp.maximum(table[0, b], 0)] - BLK * table[1, b]
        limit = jnp.where(column < 8, limit_a, limit_b)
        scores = jnp.where(position < limit, scores * SCALE, FLOOR)
        top = jnp.max(scores, axis=1, keepdims=True)
        weights = jnp.exp(scores - top)
        block_total = jnp.sum(weights, axis=1, keepdims=True)
        is_first = jnp.where(column < 8, table[1, a], table[1, b]) == 0
        own = jnp.sum(queries * of_pair(pair, G), axis=1, keepdims=True) * SCALE
        own = jnp.where(is_first, own, FLOOR)
        highest = jnp.maximum(top, own)
        factor = jnp.exp(top - highest)
        own_weight = jnp.where(is_first, jnp.exp(own - highest), 0.0)
        slot_total = block_total * factor + own_weight
        return highest, slot_total, factor, own_weight, weights.astype(BF16)

    def weigh(pair, highest, slot_total, factor, own_weight, weights):
        values = jnp.concatenate([v_v[2 * pair], v_v[2 * pair + 1]], axis=1)
        both = jnp.dot(weights, values, preferred_element_type=F32)
        block_out = jnp.where(sub16 < 8, both[:, :HD], both[:, HD:])
        slot_out = (block_out * factor + own_weight * of_pair(pair, G + 1)) / slot_total
        return slot_out.astype(BF16)

    for load in v_loads:
        load.wait()
    for c, (start, count, rows) in enumerate(CHUNKS):
        wait_bytes(recvs[c].at[others], recv_sem.at[1 + c])
        total = 0.0
        for j in range(KV):
            first, second, third = (
                sends[i].at[PEERS] if j == PEERS else recvs[i].at[j] for i in range(len(CHUNKS))
            )
            scale = jnp.exp2(first[32:48].astype(jnp.int32).astype(F32)[8:, c : c + 1]) * (1.0 / STEPS)
            if c < 2:
                got = (first, second)[c][...].astype(jnp.int32).astype(F32)[:40]
            else:
                got = jnp.concatenate(
                    [
                        second[32:48].astype(jnp.int32).astype(F32)[8:],
                        third[...].astype(jnp.int32).astype(F32),
                    ],
                    axis=0,
                )
            total = total + got.reshape(got.shape[0] // 8, 8, HD) * scale
        total = total.reshape(total.shape[0] * 8, HD)
        total = total.astype(BF16).astype(F32)
        per_tile = 8 // count
        for entry in range(ENTRIES):
            row = entry * count
            query_rows[pl.ds(16 * start + entry, count, stride=16), :] = total[row : row + count]

        pairs = range(start // 2, (start + count) // 2)
        ready = {}
        for pair in pairs:
            queries, scores = score(pair)
            ready[pair] = (queries, scores)
        for pair in pairs:
            ready[pair] = soften(pair, *ready[pair])
            highest, slot_total = ready[pair][:2]
            for s, part in ((2 * pair, slice(0, 8)), (2 * pair + 1, slice(8, 16))):
                stats = jnp.where(lane == TOP_LANES[c] + s - start, highest[part], stats)
                stats = jnp.where(lane == TOTAL_LANES[c] + s - start, slot_total[part], stats)
        if start + count == SLOTS:
            stats_all[PEERS] = stats
            for j, offset in enumerate(OFFSETS):
                send(7, stats_all.at[PEERS], stats_all.at[j], ahead(offset))
        for pair in pairs:
            at = 16 * pair - 8 * start
            outs[c][PEERS, at : at + 16, :] = weigh(pair, *ready[pair])
        for j, offset in enumerate(OFFSETS):
            send(4 + c, outs[c].at[PEERS], outs[c].at[j], ahead(offset))

    def side_by_side(tiles, shift):
        halves = [jnp.full((8, HD), -1.0, F32), jnp.full((8, HD), -1.0, F32)]
        for (start, count, _), first in zip(CHUNKS, LANES):
            for j in range(KV):
                half, at = divmod(first + count * j, HD)
                moved = pltpu.roll(tiles(j), (at - start - shift) % HD, 1)
                halves[half] = jnp.where((lane >= at) & (lane < at + count), moved, halves[half])
        return jnp.concatenate(halves, axis=1)

    owners = side_by_side(lambda j: first_all[j], OWNER_LANE)
    belongs = lax.broadcasted_iota(jnp.int32, (ROWS, 2 * HD), 0).astype(F32) == owners[0:1]

    wait_bytes(stats_all.at[others], recv_sem.at[7])
    def placed(shift, count):
        tile = jnp.full((8, HD), -1.0, F32)
        group = (lane % 64) // count
        for j in range(KV):
            tile = jnp.where(group == j, pltpu.roll(stats_all[j], (count * j - shift) % HD, 1), tile)
        return tile

    last = placed(TOP_LANES[2], 2)
    tops = jnp.concatenate([placed(TOP_LANES[0], 4), last], axis=1)
    totals = jnp.concatenate([placed(TOTAL_LANES[0], 4), pltpu.roll(last, 64, 1)], axis=1)
    shares = []
    for g in range(G):
        masked = jnp.where(belongs, tops[g : g + 1], -3e38)
        highest = jnp.max(masked, axis=1, keepdims=True)
        share = jnp.exp(masked - highest) * totals[g : g + 1]
        upper = share.astype(BF16)
        lower = (share - upper.astype(F32)).astype(BF16)
        shares.append(jnp.concatenate([upper, lower], axis=0))

    def arrived(c):
        wait_bytes(outs[c].at[others], recv_sem.at[4 + c])
        wides[c][...] = outs[c][...].astype(F32).reshape(wides[c].shape)

    def slots_of(c, g):
        return wides[c][pl.ds(g, wides[c].shape[0] // G, stride=G), :].astype(BF16)

    for c in range(len(CHUNKS)):
        arrived(c)
    ones = jnp.ones((2 * HD, HD), BF16)
    attended = []
    for g in range(G):
        slots = [slots_of(c, g) for c in sorted(range(len(CHUNKS)), key=lambda c: LANES[c])]
        slots = jnp.concatenate(slots + [jnp.zeros((2 * HD - KV * SLOTS, HD), BF16)], axis=0)
        both = jnp.dot(
            shares[g], jnp.concatenate([slots, ones], axis=1), preferred_element_type=F32
        )
        both = both[:ROWS] + both[ROWS:]
        attended.append((both[:, :HD] / both[:, HD:]).astype(BF16))
    attended = jnp.concatenate(attended, axis=1)

    loads[3].wait()
    mine = pl.ds(pl.multiple_of(core * HALF, HALF), HALF)
    theirs = pl.ds(pl.multiple_of((1 - core) * HALF, HALF), HALF)
    half_send[...] = jnp.dot(attended, w_out[:, theirs], preferred_element_type=F32)
    send(8, half_send, half_recv, sibling)
    own_half = jnp.dot(attended, w_out[:, mine], preferred_element_type=F32)
    wait_bytes(half_recv, recv_sem.at[8])
    z_all[my_z] = (own_half + half_recv[...]).astype(BF16)
    for peer in z_peers:
        send(9, z_all.at[my_z], z_all.at[my_z], peer)
    wait_bytes(first_all.at[others], send_sem.at[0])
    for c, (start, count, rows) in enumerate(CHUNKS):
        wait_bytes(sends[c].at[others], send_sem.at[1 + c])
        wait_bytes(outs[c].at[others], send_sem.at[4 + c])
    wait_bytes(stats_all.at[others], send_sem.at[7])
    wait_bytes(half_send, send_sem.at[8])
    wait_bytes(z_all.at[pl.ds(0, SIDE - 1)], recv_sem.at[9])
    parts = [z_all[z].astype(F32) for z in range(SIDE)]
    done = (((parts[0] + parts[1]) + parts[2]) + parts[3]).astype(BF16)
    done_send[...] = done
    send(10, done_send, out_ref.at[:, mine], sibling)
    out_ref[:, mine] = done
    wait_bytes(z_all.at[pl.ds(0, SIDE - 1)], send_sem.at[9])
    wait_bytes(done_send, send_sem.at[10])
    wait_bytes(out_ref.at[:, theirs], recv_sem.at[10])


def per_device(tokens, gain, w_qkv, w_out, k_cache, v_cache, lengths, block_table):
    features = tokens.shape[1]
    anywhere = pl.BlockSpec(memory_space=pl.ANY)
    return pl.pallas_call(
        kernel,
        out_shape=pltpu.VMEM((ROWS, features), BF16),
        in_specs=[anywhere] * 8,
        out_specs=pl.BlockSpec(memory_space=pltpu.VMEM),
        scratch_shapes=[
            pltpu.VMEM((ROWS, features), BF16),
            pltpu.VMEM((1, features), F32),
            pltpu.VMEM((features, ENTRIES * HD), BF16),
            pltpu.VMEM((G * HD, features), BF16),
            pltpu.VMEM((SLOTS, BLK, HD), BF16),
            pltpu.VMEM((SLOTS // 2, 2 * HD, BLK), BF16),
            pltpu.VMEM((SLOTS, BLK, HD), BF16),
            pltpu.VMEM((KV, 8, HD), F32),
        ]
        + [pltpu.VMEM((KV, rows, HD), jnp.int16) for _, _, rows in CHUNKS]
        + [pltpu.VMEM((PEERS, rows, HD), jnp.int16) for _, _, rows in CHUNKS]
        + [
            pltpu.VMEM((18 * 16, HD), F32),
        ]
        + [pltpu.VMEM((KV, count * G, HD), BF16) for _, count, _ in CHUNKS]
        + [pltpu.VMEM((KV, 8, HD), F32)]
        + [pltpu.VMEM((KV * count * G, HD), F32) for _, count, _ in CHUNKS]
        + [
            pltpu.VMEM((ROWS, HALF), F32),
            pltpu.VMEM((ROWS, HALF), F32),
            pltpu.VMEM((SIDE, ROWS, HALF), BF16),
            pltpu.VMEM((ROWS, HALF), BF16),
            pltpu.SMEM((ROWS,), jnp.int32),
            pltpu.SMEM((2, SLOTS), jnp.int32),
            pltpu.SemaphoreType.DMA((6,)),
            pltpu.SemaphoreType.DMA((2, SLOTS // 2)),
            pltpu.SemaphoreType.DMA((11,)),
            pltpu.SemaphoreType.DMA((11,)),
        ],
        compiler_params=pltpu.CompilerParams(
            collective_id=0, has_side_effects=True, vmem_limit_bytes=56 << 20
        ),
    )(
        tokens,
        gain.reshape(1, features),
        w_qkv.reshape(features, ENTRIES * HD),
        w_out.reshape(G * HD, features),
        k_cache.reshape(SLOTS, BLK, HD),
        v_cache.reshape(SLOTS, BLK, HD),
        lengths,
        block_table.T,
    )


def solution(mesh):
    placed = (
        P(None, "kv"),
        P("kv"),
        P("kv", "tp", None),
        P("tp", None, "kv"),
        P("tp", "kv", None, None),
        P("tp", "kv", None, None),
        P(),
        P("kv", None),
    )
    return jax.shard_map(
        per_device, mesh=mesh, in_specs=placed, out_specs=P(None, "kv"), check_vma=False
    )
```

```python
import functools

import jax
import jax.numpy as jnp
from jax import lax
from jax.experimental import pallas as pl
from jax.experimental.pallas import tpu as pltpu
from jax.sharding import PartitionSpec as P

D = 8192
HD = 128
G = 8
ROWS = 64
SLOTS = 10
ENTRIES = G + 2
BLK = 4096
SIDE = 4
KV = SIDE * SIDE
PEERS = KV - 1
HALF = 256

EPSILON = 1e-05
FLOOR = -1e30
SCALE = HD ** (-0.5)

MESH = pl.DeviceIdType.MESH
F32 = jnp.float32
BF16 = jnp.bfloat16

SQUARE_LANE = 8
OWNER_LANE = 16

EARLY_VALUES = 1
EARLY_KEYS = 2
TURN = 512

CHUNKS = ((0, 4, 48), (4, 4, 48), (8, 2, 16))
LANES = (0, 64, 128)
TOP_LANES = (0, 64, 32)
TOTAL_LANES = (16, 80, 96)

STEPS = 32000.0


def ring_distance(step):
    return min(step, SIDE - step)


OFFSETS = sorted(
    [(a, b) for a in range(SIDE) for b in range(SIDE) if (a, b) != (0, 0)],
    key=lambda m: -(ring_distance(m[0]) + ring_distance(m[1])),
)


def wait_bytes(ref, sem):
    pltpu.make_async_copy(ref, ref, sem).wait()


def kernel(
    tokens_hbm,
    gain_hbm,
    w_qkv_hbm,
    w_out_hbm,
    k_hbm,
    v_hbm,
    lengths_hbm,
    table_hbm,
    out_ref,
    tokens_v,
    gain_v,
    w_qkv,
    w_out,
    k_v,
    k_turned,
    v_v,
    first_all,
    send0,
    send1,
    send2,
    recv0,
    recv1,
    recv2,
    query_rows,
    outs0,
    outs1,
    outs2,
    stats_all,
    wide0,
    wide1,
    wide2,
    half_send,
    half_recv,
    z_all,
    done_send,
    lengths,
    table,
    load_sem,
    kv_sem,
    send_sem,
    recv_sem,
):
    me = lax.axis_index("kv")
    my_x, my_y = me // SIDE, me % SIDE
    tp = lax.axis_index("tp")
    my_z, core = tp // 2, tp % 2

    def ahead(offset):
        return {"kv": ((my_x + offset[0]) % SIDE) * SIDE + (my_y + offset[1]) % SIDE}

    def behind(offset):
        return ahead(((SIDE - offset[0]) % SIDE, (SIDE - offset[1]) % SIDE))

    sibling = {"tp": my_z * 2 + (1 - core)}
    z_peers = [{"tp": ((my_z + step) % SIDE) * 2 + core} for step in (2, 1, 3)]

    barrier = pltpu.get_barrier_semaphore()
    for offset in OFFSETS:
        pl.semaphore_signal(barrier, inc=1, device_id=ahead(offset), device_id_type=MESH)
    for peer in z_peers + [sibling]:
        pl.semaphore_signal(barrier, inc=1, device_id=peer, device_id_type=MESH)

    loads = [
        pltpu.make_async_copy(tokens_hbm, tokens_v, load_sem.at[0]),
        pltpu.make_async_copy(gain_hbm, gain_v, load_sem.at[1]),
        pltpu.make_async_copy(w_qkv_hbm, w_qkv, load_sem.at[2]),
        pltpu.make_async_copy(w_out_hbm, w_out, load_sem.at[3]),
        pltpu.make_async_copy(table_hbm, table, load_sem.at[4]),
        pltpu.make_async_copy(lengths_hbm, lengths, load_sem.at[5]),
    ]
    k_loads, v_loads = [], []
    for pair in range(SLOTS // 2):
        part = pl.ds(2 * pair, 2)
        k_loads.append(pltpu.make_async_copy(k_hbm.at[part], k_v.at[part], kv_sem.at[0, pair]))
        v_loads.append(pltpu.make_async_copy(v_hbm.at[part], v_v.at[part], kv_sem.at[1, pair]))
    for load in loads[:3] + loads[4:]:
        load.start()
    for pair in range(SLOTS // 2):
        k_loads[pair].start()
    for pair in range(EARLY_VALUES):
        v_loads[pair].start()

    sub = lax.broadcasted_iota(jnp.int32, (8, HD), 0)
    lane = lax.broadcasted_iota(jnp.int32, (8, HD), 1)

    loads[0].wait()
    tokens = tokens_v[...].astype(F32)
    squares = jnp.sum(tokens * tokens, axis=1, keepdims=True)
    loads[4].wait()
    loads[5].wait()
    owners = jnp.full((8, HD), -1, jnp.int32)
    for slot in range(SLOTS):
        owners = jnp.where(lane == OWNER_LANE + slot, table[0, slot], owners)
    for c, (start, count, _) in enumerate(CHUNKS):
        for s in range(count):
            owners = jnp.where((lane == c) & (sub % count == s), table[0, start + s], owners)
    tile = owners.astype(F32)
    for k in range(ROWS // 8):
        tile = jnp.where(lane == SQUARE_LANE + k, squares[8 * k : 8 * k + 8], tile)
    first_all[PEERS] = tile

    pl.semaphore_wait(barrier, PEERS + 4)

    def send(phase, src, dst, peer):
        pltpu.make_async_remote_copy(
            src_ref=src,
            dst_ref=dst,
            send_sem=send_sem.at[phase],
            recv_sem=recv_sem.at[phase],
            device_id=peer,
            device_id_type=MESH,
        ).start()

    others = pl.ds(0, PEERS)

    for j, offset in enumerate(OFFSETS):
        send(0, first_all.at[PEERS], first_all.at[j], ahead(offset))

    def turn_keys(pair):
        k_loads[pair].wait()
        for half in range(2):
            for at in range(0, BLK, TURN):
                k_turned[pair, HD * half : HD * half + HD, at : at + TURN] = k_v[
                    2 * pair + half, at : at + TURN
                ].T

    for pair in range(EARLY_KEYS):
        turn_keys(pair)
    loads[1].wait()
    loads[2].wait()
    wait_bytes(first_all.at[others], recv_sem.at[0])

    for pair in range(EARLY_VALUES, SLOTS // 2):
        v_loads[pair].start()
    loads[3].start()
    squares = first_all[0]
    for j in range(1, KV):
        squares = squares + first_all[j]
    inverse = lax.rsqrt(squares / D + EPSILON)
    gains = gain_v[...]
    normed = jnp.concatenate(
        [tokens[8 * k : 8 * k + 8] * inverse[:, SQUARE_LANE + k : SQUARE_LANE + k + 1] * gains for k in range(ROWS // 8)], axis=0
    ).astype(BF16)
    partial = jnp.dot(normed, w_qkv[...], preferred_element_type=F32)
    largest = jnp.max(jnp.abs(partial), axis=1, keepdims=True)
    exponent = jnp.ceil(jnp.log2(jnp.maximum(largest, 1e-30)))
    whole = jnp.round(partial * (STEPS * jnp.exp2(-exponent)))
    coarse = jnp.floor(whole * (1.0 / 256.0))
    fine = whole - 256.0 * coarse
    stacked = jnp.concatenate([coarse, fine], axis=0).astype(BF16)
    exponents = jnp.broadcast_to(exponent, (ROWS, HD))
    exponents = jnp.concatenate([jnp.zeros_like(exponents), exponents], axis=0).astype(BF16)

    row_of_lane = lax.broadcasted_iota(jnp.int32, (KV * 8, HD), 1)
    row_number = (row_of_lane % ROWS).astype(F32)
    part_weight = jnp.where(row_of_lane < ROWS, 256.0, 1.0)
    everyone = first_all[...].reshape(KV * 8, HD)
    sub3 = lax.broadcasted_iota(jnp.int32, (KV, 8, HD), 1)
    sends = (send0, send1, send2)
    recvs = (recv0, recv1, recv2)
    outs = (outs0, outs1, outs2)
    wides = (wide0, wide1, wide2)
    picks = [
        jnp.where(everyone[:, c : c + 1] == row_number, part_weight, 0.0).astype(BF16)
        for c in range(len(CHUNKS))
    ]

    def packed(c):
        _, count, _ = CHUNKS[c]
        got = jnp.dot(picks[c], stacked, preferred_element_type=F32).reshape(KV, 8, ENTRIES * HD)
        per_tile = 8 // count
        tiles = []
        for first in range(0, ENTRIES, per_tile):
            tile = got[:, :, first * HD : (first + 1) * HD]
            for e in range(1, min(per_tile, ENTRIES - first)):
                tile = jnp.where(
                    sub3 >= e * count, got[:, :, (first + e) * HD : (first + e + 1) * HD], tile
                )
            tiles.append(tile)
        return tiles

    def send_rows(c, tiles):
        sends[c][...] = jnp.concatenate(tiles, axis=1).astype(jnp.int32).astype(jnp.int16)
        for j, offset in enumerate(OFFSETS):
            send(1 + c, sends[c].at[j], recvs[c].at[j], behind(offset))

    lane3 = lax.broadcasted_iota(jnp.int32, (KV, 8, HD), 2)
    marks = jnp.zeros((KV, 8, HD), F32)
    for c, pick in enumerate(picks):
        mark = jnp.dot(pick, exponents, preferred_element_type=F32).reshape(KV, 8, HD)
        marks = jnp.where(lane3 == c, mark, marks)
    send_rows(0, packed(0) + [marks])
    last_tiles = packed(2)
    send_rows(1, packed(1) + last_tiles[:1])
    send_rows(2, last_tiles[1:])

    for pair in range(EARLY_KEYS, SLOTS // 2):
        turn_keys(pair)

    sub16 = lax.broadcasted_iota(jnp.int32, (16, HD), 0)
    column = lax.broadcasted_iota(jnp.int32, (16, 1), 0)
    position = lax.broadcasted_iota(jnp.int32, (16, BLK), 1)
    stats = jnp.zeros((8, HD), F32)

    def of_pair(pair, entry):
        a, b = 32 * pair + entry, 32 * pair + 16 + entry
        return jnp.where(sub16 < 8, query_rows[a : a + 1, :], query_rows[b : b + 1, :])

    def score(pair):
        a, b = 32 * pair, 32 * pair + 16
        queries = jnp.concatenate([query_rows[a : a + G, :], query_rows[b : b + G, :]], axis=0)
        left = jnp.concatenate(
            [jnp.where(sub16 < 8, queries, 0.0), jnp.where(sub16 < 8, 0.0, queries)], axis=1
        ).astype(BF16)
        return queries, jnp.dot(left, k_turned[pair], preferred_element_type=F32)

    def soften(pair, queries, scores):
        a, b = 2 * pair, 2 * pair + 1
        limit_a = lengths[jnp.maximum(table[0, a], 0)] - BLK * table[1, a]
        limit_b = lengths[jnp.maximum(table[0, b], 0)] - BLK * table[1, b]
        limit = jnp.where(column < 8, limit_a, limit_b)
        scores = jnp.where(position < limit, scores * SCALE, FLOOR)
        top = jnp.max(scores, axis=1, keepdims=True)
        weights = jnp.exp(scores - top)
        block_total = jnp.sum(weights, axis=1, keepdims=True)
        is_first = jnp.where(column < 8, table[1, a], table[1, b]) == 0
        own = jnp.sum(queries * of_pair(pair, G), axis=1, keepdims=True) * SCALE
        own = jnp.where(is_first, own, FLOOR)
        highest = jnp.maximum(top, own)
        factor = jnp.exp(top - highest)
        own_weight = jnp.where(is_first, jnp.exp(own - highest), 0.0)
        slot_total = block_total * factor + own_weight
        return highest, slot_total, factor, own_weight, weights.astype(BF16)

    def weigh(pair, highest, slot_total, factor, own_weight, weights):
        values = jnp.concatenate([v_v[2 * pair], v_v[2 * pair + 1]], axis=1)
        both = jnp.dot(weights, values, preferred_element_type=F32)
        block_out = jnp.where(sub16 < 8, both[:, :HD], both[:, HD:])
        slot_out = (block_out * factor + own_weight * of_pair(pair, G + 1)) / slot_total
        return slot_out.astype(BF16)

    for load in v_loads:
        load.wait()
    for c, (start, count, rows) in enumerate(CHUNKS):
        wait_bytes(recvs[c].at[others], recv_sem.at[1 + c])
        total = 0.0
        for j in range(KV):
            first, second, third = (
                sends[i].at[PEERS] if j == PEERS else recvs[i].at[j] for i in range(len(CHUNKS))
            )
            scale = jnp.exp2(first[32:48].astype(jnp.int32).astype(F32)[8:, c : c + 1]) * (1.0 / STEPS)
            if c < 2:
                got = (first, second)[c][...].astype(jnp.int32).astype(F32)[:40]
            else:
                got = jnp.concatenate(
                    [
                        second[32:48].astype(jnp.int32).astype(F32)[8:],
                        third[...].astype(jnp.int32).astype(F32),
                    ],
                    axis=0,
                )
            total = total + got.reshape(got.shape[0] // 8, 8, HD) * scale
        total = total.reshape(total.shape[0] * 8, HD)
        total = total.astype(BF16).astype(F32)
        per_tile = 8 // count
        for entry in range(ENTRIES):
            row = entry * count
            query_rows[pl.ds(16 * start + entry, count, stride=16), :] = total[row : row + count]

        pairs = range(start // 2, (start + count) // 2)
        ready = {}
        for pair in pairs:
            queries, scores = score(pair)
            ready[pair] = (queries, scores)
        for pair in pairs:
            ready[pair] = soften(pair, *ready[pair])
            highest, slot_total = ready[pair][:2]
            for s, part in ((2 * pair, slice(0, 8)), (2 * pair + 1, slice(8, 16))):
                stats = jnp.where(lane == TOP_LANES[c] + s - start, highest[part], stats)
                stats = jnp.where(lane == TOTAL_LANES[c] + s - start, slot_total[part], stats)
        if start + count == SLOTS:
            stats_all[PEERS] = stats
            for j, offset in enumerate(OFFSETS):
                send(7, stats_all.at[PEERS], stats_all.at[j], ahead(offset))
        for pair in pairs:
            at = 16 * pair - 8 * start
            outs[c][PEERS, at : at + 16, :] = weigh(pair, *ready[pair])
        for j, offset in enumerate(OFFSETS):
            send(4 + c, outs[c].at[PEERS], outs[c].at[j], ahead(offset))

    def side_by_side(tiles, shift):
        halves = [jnp.full((8, HD), -1.0, F32), jnp.full((8, HD), -1.0, F32)]
        for (start, count, _), first in zip(CHUNKS, LANES):
            for j in range(KV):
                half, at = divmod(first + count * j, HD)
                moved = pltpu.roll(tiles(j), (at - start - shift) % HD, 1)
                halves[half] = jnp.where((lane >= at) & (lane < at + count), moved, halves[half])
        return jnp.concatenate(halves, axis=1)

    owners = side_by_side(lambda j: first_all[j], OWNER_LANE)
    belongs = lax.broadcasted_iota(jnp.int32, (ROWS, 2 * HD), 0).astype(F32) == owners[0:1]

    wait_bytes(stats_all.at[others], recv_sem.at[7])
    def placed(shift, count):
        tile = jnp.full((8, HD), -1.0, F32)
        group = (lane % 64) // count
        for j in range(KV):
            tile = jnp.where(group == j, pltpu.roll(stats_all[j], (count * j - shift) % HD, 1), tile)
        return tile

    last = placed(TOP_LANES[2], 2)
    tops = jnp.concatenate([placed(TOP_LANES[0], 4), last], axis=1)
    totals = jnp.concatenate([placed(TOTAL_LANES[0], 4), pltpu.roll(last, 64, 1)], axis=1)
    shares = []
    for g in range(G):
        masked = jnp.where(belongs, tops[g : g + 1], -3e38)
        highest = jnp.max(masked, axis=1, keepdims=True)
        share = jnp.exp(masked - highest) * totals[g : g + 1]
        upper = share.astype(BF16)
        lower = (share - upper.astype(F32)).astype(BF16)
        shares.append(jnp.concatenate([upper, lower], axis=0))

    def arrived(c):
        wait_bytes(outs[c].at[others], recv_sem.at[4 + c])
        wides[c][...] = outs[c][...].astype(F32).reshape(wides[c].shape)

    def slots_of(c, g):
        return wides[c][pl.ds(g, wides[c].shape[0] // G, stride=G), :].astype(BF16)

    for c in range(len(CHUNKS)):
        arrived(c)
    ones = jnp.ones((2 * HD, HD), BF16)
    attended = []
    for g in range(G):
        slots = [slots_of(c, g) for c in sorted(range(len(CHUNKS)), key=lambda c: LANES[c])]
        slots = jnp.concatenate(slots + [jnp.zeros((2 * HD - KV * SLOTS, HD), BF16)], axis=0)
        both = jnp.dot(
            shares[g], jnp.concatenate([slots, ones], axis=1), preferred_element_type=F32
        )
        both = both[:ROWS] + both[ROWS:]
        attended.append((both[:, :HD] / both[:, HD:]).astype(BF16))
    attended = jnp.concatenate(attended, axis=1)

    loads[3].wait()
    mine = pl.ds(pl.multiple_of(core * HALF, HALF), HALF)
    theirs = pl.ds(pl.multiple_of((1 - core) * HALF, HALF), HALF)
    half_send[...] = jnp.dot(attended, w_out[:, theirs], preferred_element_type=F32)
    send(8, half_send, half_recv, sibling)
    own_half = jnp.dot(attended, w_out[:, mine], preferred_element_type=F32)
    wait_bytes(half_recv, recv_sem.at[8])
    z_all[my_z] = (own_half + half_recv[...]).astype(BF16)
    for peer in z_peers:
        send(9, z_all.at[my_z], z_all.at[my_z], peer)
    wait_bytes(first_all.at[others], send_sem.at[0])
    for c, (start, count, rows) in enumerate(CHUNKS):
        wait_bytes(sends[c].at[others], send_sem.at[1 + c])
        wait_bytes(outs[c].at[others], send_sem.at[4 + c])
    wait_bytes(stats_all.at[others], send_sem.at[7])
    wait_bytes(half_send, send_sem.at[8])
    wait_bytes(z_all.at[pl.ds(0, SIDE - 1)], recv_sem.at[9])
    parts = [z_all[z].astype(F32) for z in range(SIDE)]
    done = (((parts[0] + parts[1]) + parts[2]) + parts[3]).astype(BF16)
    done_send[...] = done
    send(10, done_send, out_ref.at[:, mine], sibling)
    out_ref[:, mine] = done
    wait_bytes(z_all.at[pl.ds(0, SIDE - 1)], send_sem.at[9])
    wait_bytes(done_send, send_sem.at[10])
    wait_bytes(out_ref.at[:, theirs], recv_sem.at[10])


def per_device(tokens, gain, w_qkv, w_out, k_cache, v_cache, lengths, block_table):
    features = tokens.shape[1]
    anywhere = pl.BlockSpec(memory_space=pl.ANY)
    return pl.pallas_call(
        kernel,
        out_shape=pltpu.VMEM((ROWS, features), BF16),
        in_specs=[anywhere] * 8,
        out_specs=pl.BlockSpec(memory_space=pltpu.VMEM),
        scratch_shapes=[
            pltpu.VMEM((ROWS, features), BF16),
            pltpu.VMEM((1, features), F32),
            pltpu.VMEM((features, ENTRIES * HD), BF16),
            pltpu.VMEM((G * HD, features), BF16),
            pltpu.VMEM((SLOTS, BLK, HD), BF16),
            pltpu.VMEM((SLOTS // 2, 2 * HD, BLK), BF16),
            pltpu.VMEM((SLOTS, BLK, HD), BF16),
            pltpu.VMEM((KV, 8, HD), F32),
        ]
        + [pltpu.VMEM((KV, rows, HD), jnp.int16) for _, _, rows in CHUNKS]
        + [pltpu.VMEM((PEERS, rows, HD), jnp.int16) for _, _, rows in CHUNKS]
        + [
            pltpu.VMEM((18 * 16, HD), F32),
        ]
        + [pltpu.VMEM((KV, count * G, HD), BF16) for _, count, _ in CHUNKS]
        + [pltpu.VMEM((KV, 8, HD), F32)]
        + [pltpu.VMEM((KV * count * G, HD), F32) for _, count, _ in CHUNKS]
        + [
            pltpu.VMEM((ROWS, HALF), F32),
            pltpu.VMEM((ROWS, HALF), F32),
            pltpu.VMEM((SIDE, ROWS, HALF), BF16),
            pltpu.VMEM((ROWS, HALF), BF16),
            pltpu.SMEM((ROWS,), jnp.int32),
            pltpu.SMEM((2, SLOTS), jnp.int32),
            pltpu.SemaphoreType.DMA((6,)),
            pltpu.SemaphoreType.DMA((2, SLOTS // 2)),
            pltpu.SemaphoreType.DMA((11,)),
            pltpu.SemaphoreType.DMA((11,)),
        ],
        compiler_params=pltpu.CompilerParams(
            collective_id=0, has_side_effects=True, vmem_limit_bytes=56 << 20
        ),
    )(
        tokens,
        gain.reshape(1, features),
        w_qkv.reshape(features, ENTRIES * HD),
        w_out.reshape(G * HD, features),
        k_cache.reshape(SLOTS, BLK, HD),
        v_cache.reshape(SLOTS, BLK, HD),
        lengths,
        block_table.T,
    )


def solution(mesh):
    placed = (
        P(None, "kv"),
        P("kv"),
        P("kv", "tp", None),
        P("tp", None, "kv"),
        P("tp", "kv", None, None),
        P("tp", "kv", None, None),
        P(),
        P("kv", None),
    )
    return jax.shard_map(
        per_device, mesh=mesh, in_specs=placed, out_specs=P(None, "kv"), check_vma=False
    )
```
